32 devices in a mesh: pool: 4 (over x, core), frame: 2 (over y), tensor: 4 (over z).
Axes of the slice: x: 2, y: 2, z: 4, core: 2. Of those that a mesh axis runs over, the one named last changes fastest.
Arguments:
- latents: bfloat16 [4096, 2240], P(('pool', 'frame', 'tensor')), parts along dimension 0, may hold values from -6 to 6
- queries: bfloat16 [4096, 2240], P(('pool', 'frame'), 'tensor'), parts along dimension 0, may hold values from -6 to 6
- keys: bfloat16 [4096, 2240], P(('pool', 'frame'), 'tensor'), parts along dimension 0, may hold values from -6 to 6
- values: bfloat16 [4096, 2240], P(('pool', 'frame'), 'tensor'), parts along dimension 0, may hold values from -6 to 6
- log_decay: float32 [20, 4096], P('tensor', ('pool', 'frame')), parts along dimension 1, may hold values from -0.6 to 0, as said below
- block_ids: int32 [4096], P(('pool', 'frame')), parts along dimension 0, may hold values from 0 to 3, as said below
- t_index: int32 [4], P('pool'), parts along dimension 0, may hold values from 0 to 49
- w_mod: bfloat16 [256, 8960], replicated, may hold values from -0.375 to 0.375
- w_out: bfloat16 [2240, 2240], P('tensor', 'frame'), may hold values from -0.125 to 0.125
- w_up: bfloat16 [2240, 4480], P('frame', 'tensor'), may hold values from -0.125 to 0.125
- w_down: bfloat16 [4480, 2240], P('tensor', 'frame'), may hold values from -0.09375 to 0.09375
Outputs:
- velocity: bfloat16 [4096, 2240], P(('pool', 'frame', 'tensor')), parts along dimension 0
- advanced: bfloat16 [4096, 2240], P(('pool', 'frame', 'tensor')), parts along dimension 0
The draws below stay inside these ranges and needn't reach their ends.
There are 4 independent parts, one for each index of `pool`. The reference program is written for one: setup_inputs(seed, part) draws one part's arguments, and reference() takes and returns one part's arrays. A program takes and returns all parts, laid end to end along the dimension named above; an argument that names none is the same for every part. Nothing has to cross between parts.
Inputs may be any that keep to these rules, and one draw needn't show every extreme that they name: `block_ids`: within each span of 512 tokens the value never falls, starts at 0 and ends at 3. `log_decay`: every entry is negative.
All inputs are finite; a program needn't handle non-finite values.
Results may differ from the reference program's by a relative error of at most 0.0085.
Values may be sent and summed in bfloat16 or wider, within the bound.
A program may use at most 128 MiB of HBM per device.

```python
import math
import jax
import jax.numpy as jnp
from jax import lax

D = 2240
ATTENTION_HEADS = 20
DH = 112
FFW = 4480
TEMB = 256
STEPS = 50
SUBS = 4
TOK_DEV = 512
SAMPLE_TOKENS = 1024
HD = 2240
N_FRAME = 2
N_TENSOR = 4


def draw_log_decay(key, part):
    random_subkeys = jax.random.split(key, 7)
    block_count = SAMPLE_TOKENS // TOK_DEV
    quick_share = 0.5
    quick_heads = jax.random.uniform(random_subkeys[0], (ATTENTION_HEADS, 1)) < quick_share
    quick_rate = jax.random.uniform(random_subkeys[1], (ATTENTION_HEADS, 1), minval=1.0 / 50.0, maxval=1.0 / 30.0)
    slow_rate = jax.random.uniform(random_subkeys[2], (ATTENTION_HEADS, 1), minval=0.1, maxval=0.3) / SAMPLE_TOKENS
    spread = jnp.exp(jax.random.uniform(random_subkeys[3], (ATTENTION_HEADS, block_count), minval=-math.log(2.0), maxval=math.log(2.0)))
    spread = jnp.repeat(spread, TOK_DEV, axis=1)
    roughness = jax.random.uniform(random_subkeys[4], (ATTENTION_HEADS, SAMPLE_TOKENS), minval=0.5, maxval=1.5)
    decay_speed = jnp.where(quick_heads, quick_rate, slow_rate) * spread * roughness
    spike_locations = jax.random.randint(random_subkeys[5], (3,), 0, SAMPLE_TOKENS)
    spike_mask = jnp.any(jnp.arange(SAMPLE_TOKENS)[None, :] == spike_locations[:, None], axis=0)
    spike_logarithm = jnp.log(jax.random.uniform(random_subkeys[6], (ATTENTION_HEADS, SAMPLE_TOKENS), minval=0.65, maxval=0.8))
    return (-decay_speed + jnp.where(spike_mask[None, :], spike_logarithm, 0.0)).astype(jnp.float32)


def draw_block_ids(key, part):
    block_count = SAMPLE_TOKENS // TOK_DEV
    cut_points = jax.random.randint(key, (block_count, 1, SUBS - 1), 1, TOK_DEV)
    places = jnp.arange(TOK_DEV).astype(jnp.int32)
    labels = jnp.sum((places[None, :, None] >= cut_points).astype(jnp.int32), axis=2)
    return labels.reshape(SAMPLE_TOKENS).astype(jnp.int32)


def levels(rng, extent, shards, least, top_value):
    level = 1.0
    for axis_at, shards_of in shards:
        heights = jax.random.uniform(jax.random.fold_in(jax.random.fold_in(rng, 6), axis_at), (shards_of,), jnp.float32, least / len(shards), top_value / len(shards))
        level = level * jnp.repeat(jnp.exp(heights), extent[axis_at] // shards_of).reshape((-1,) + (1,) * (len(extent) - 1 - axis_at))
    return level


def gaussian(rng, extent, deviation, bound, pieces=(), held_as=jnp.bfloat16):
    gain = levels(rng, extent, pieces, -0.22, 0.18) if pieces else 1.0
    values = jax.random.normal(rng, extent, jnp.float32) * deviation * gain
    return jnp.minimum(jnp.maximum(values, -bound), bound).astype(held_as)


def setup_inputs(seed: int = 0, part: int = 0) -> dict:
    arg_keys = jax.random.split(jax.random.key(seed), 12)
    own_keys = jax.random.split(jax.random.fold_in(arg_keys[11], part), 12)
    latents = gaussian(own_keys[0], (SAMPLE_TOKENS, D), 1.0, 6.0, ((0, 8),))
    queries = gaussian(own_keys[1], (SAMPLE_TOKENS, HD), 1.0, 6.0, ((0, 2), (1, 4)))
    keys = gaussian(own_keys[2], (SAMPLE_TOKENS, HD), 1.0, 6.0, ((0, 2), (1, 4)))
    values = gaussian(own_keys[3], (SAMPLE_TOKENS, HD), 1.0, 6.0, ((0, 2), (1, 4)))
    log_decay = draw_log_decay(jax.random.fold_in(jax.random.fold_in(arg_keys[11], part), 71), part)
    block_ids = draw_block_ids(jax.random.fold_in(jax.random.fold_in(arg_keys[11], part), 71), part)
    t_index = jax.random.randint(own_keys[6], (1,), 0, STEPS).astype(jnp.int32)
    w_mod = gaussian(arg_keys[7], (TEMB, 4 * D), TEMB ** -0.5, 0.375)
    w_out = gaussian(arg_keys[8], (HD, D), HD ** -0.5, 0.125, ((0, 4), (1, 2)))
    w_up = gaussian(arg_keys[9], (D, FFW), D ** -0.5, 0.125, ((0, 2), (1, 4)))
    w_down = gaussian(arg_keys[10], (FFW, D), FFW ** -0.5, 0.09375, ((0, 4), (1, 2)))
    return {"latents": latents, "queries": queries, "keys": keys, "values": values, "log_decay": log_decay, "block_ids": block_ids, "t_index": t_index, "w_mod": w_mod, "w_out": w_out, "w_up": w_up, "w_down": w_down}


def modulation_of(t_index, w_mod):
    fraction = 1.0 - t_index[0].astype(jnp.float32) / STEPS
    following = fraction - 1.0 / STEPS
    sigma_now = 3.0 * fraction / (1.0 + 2.0 * fraction)
    sigma_next = 3.0 * following / (1.0 + 2.0 * following)
    half_width = w_mod.shape[0] // 2
    frequency = jnp.exp(-math.log(10000.0) * jnp.arange(half_width).astype(jnp.float32) / half_width)
    angles = 1000.0 * sigma_now * frequency
    embedding = jnp.concatenate([jnp.cos(angles), jnp.sin(angles)])
    time_features = jax.nn.silu(embedding).astype(jnp.bfloat16)
    shifts = jnp.dot(time_features[None, :], w_mod, preferred_element_type=jnp.float32)[0]
    return (shifts, sigma_next - sigma_now)

def own_state(key_heads, value_heads, cumulative):
    block_total = cumulative[:, -1]
    scaled = key_heads.astype(jnp.float32) * jnp.exp(block_total[:, None] - cumulative)[:, :, None]
    state_sum = jnp.einsum('htd,hte->hde', scaled, value_heads.astype(jnp.float32), precision=lax.Precision.HIGHEST)
    return (block_total, state_sum)

def mix_block(query_heads, key_heads, value_heads, cumulative, labels, carried_state):
    factor = query_heads.shape[2] ** (-0.5)
    visible = labels[None, :] <= labels[:, None]
    decay = jnp.exp(jnp.minimum(cumulative[:, :, None] - cumulative[:, None, :], 0.0))
    weights = jnp.where(visible[None], decay, 0.0) * factor
    scores = jnp.einsum('hid,hjd->hij', query_heads.astype(jnp.float32), key_heads.astype(jnp.float32))
    probs = (scores * weights).astype(jnp.bfloat16)
    inner_part = jnp.einsum('hij,hjd->hid', probs.astype(jnp.float32), value_heads.astype(jnp.float32))
    carried = jnp.einsum('hid,hde->hie', query_heads.astype(jnp.float32), carried_state, precision=lax.Precision.HIGHEST)
    numerator = inner_part + carried * (jnp.exp(cumulative) * factor)[:, :, None]
    normed = numerator * lax.rsqrt(lax.optimization_barrier(jnp.mean(numerator * numerator, axis=2, keepdims=True)) + 1e-06)
    return normed.astype(jnp.bfloat16)

def layer_norm(hidden):
    centered = hidden - lax.optimization_barrier(jnp.mean(hidden, axis=1, keepdims=True))
    variance = lax.optimization_barrier(jnp.mean(centered * centered, axis=1, keepdims=True))
    return centered * lax.rsqrt(variance + 1e-06)

def reference(latents, queries, keys, values, log_decay, block_ids, t_index, w_mod, w_out, w_up, w_down):
    shifts, step_size = modulation_of(t_index, w_mod)
    width = latents.shape[1]
    query_blocks = queries.reshape(N_FRAME, TOK_DEV, ATTENTION_HEADS, DH).transpose(0, 2, 1, 3)
    key_blocks = keys.reshape(N_FRAME, TOK_DEV, ATTENTION_HEADS, DH).transpose(0, 2, 1, 3)
    value_blocks = values.reshape(N_FRAME, TOK_DEV, ATTENTION_HEADS, DH).transpose(0, 2, 1, 3)
    decay_blocks = log_decay.reshape(ATTENTION_HEADS, N_FRAME, TOK_DEV).transpose(1, 0, 2)
    label_blocks = block_ids.reshape(N_FRAME, TOK_DEV)

    def advance(carried_state, inputs):
        query_heads, key_heads, value_heads, decay_rows, labels = inputs
        cumulative = jnp.cumsum(decay_rows, axis=1)
        mixed = mix_block(query_heads, key_heads, value_heads, cumulative, labels, carried_state)
        block_total, state_sum = own_state(key_heads, value_heads, cumulative)
        following = jnp.exp(block_total)[:, None, None] * carried_state + state_sum
        return (following, mixed)
    initial = jnp.zeros((ATTENTION_HEADS, DH, DH), jnp.float32)
    final_state, mixed_blocks = lax.scan(advance, initial, (query_blocks, key_blocks, value_blocks, decay_blocks, label_blocks))
    heads_out = mixed_blocks.transpose(0, 2, 1, 3).reshape(SAMPLE_TOKENS, ATTENTION_HEADS * DH)
    group_heads = ATTENTION_HEADS * DH // N_TENSOR
    attention = jnp.zeros((SAMPLE_TOKENS, width), jnp.float32)
    for group in range(N_TENSOR):
        partial_sum = jnp.dot(heads_out[:, group * group_heads:(group + 1) * group_heads], w_out[group * group_heads:(group + 1) * group_heads], preferred_element_type=jnp.float32)
        attention = attention + lax.optimization_barrier(partial_sum.astype(jnp.bfloat16)).astype(jnp.float32)
    hidden = latents.astype(jnp.float32) + shifts[3 * width:] * attention
    normed = (layer_norm(hidden) * (1.0 + shifts[width:2 * width]) + shifts[:width]).astype(jnp.bfloat16)
    units = jax.nn.gelu(jnp.dot(normed, w_up, preferred_element_type=jnp.float32), approximate=True).astype(jnp.bfloat16)
    group_units = FFW // N_TENSOR
    feed = jnp.zeros((SAMPLE_TOKENS, width), jnp.float32)
    for group in range(N_TENSOR):
        partial_sum = jnp.dot(units[:, group * group_units:(group + 1) * group_units], w_down[group * group_units:(group + 1) * group_units], preferred_element_type=jnp.float32)
        feed = feed + lax.optimization_barrier(partial_sum.astype(jnp.bfloat16)).astype(jnp.float32)
    velocity = (hidden + shifts[2 * width:3 * width] * feed).astype(jnp.bfloat16)
    advanced = (latents.astype(jnp.float32) + step_size * velocity.astype(jnp.float32)).astype(jnp.bfloat16)
    return (velocity, advanced)
```

```python
import functools
import math

import jax
import jax.numpy as jnp
from jax import lax
from jax.experimental import pallas as pl
from jax.experimental.pallas import tpu as pltpu
from jax.sharding import PartitionSpec as P

STEPS = 50


def shifted(block, axis, distance):
    devices = range(lax.axis_size(axis))
    route = [(i - distance, i) for i in devices if i - distance in devices]
    return lax.ppermute(block, axis, route)


def modulation_of(t_index, w_mod):
    fraction = 1.0 - t_index[0].astype(jnp.float32) / STEPS
    following = fraction - 1.0 / STEPS
    sigma_now = 3.0 * fraction / (1.0 + 2.0 * fraction)
    sigma_next = 3.0 * following / (1.0 + 2.0 * following)
    half_width = w_mod.shape[0] // 2
    frequency = jnp.exp(
        -math.log(10000.0) * jnp.arange(half_width).astype(jnp.float32) / half_width
    )
    angles = 1000.0 * sigma_now * frequency
    embedding = jnp.concatenate([jnp.cos(angles), jnp.sin(angles)])
    time_features = jax.nn.silu(embedding).astype(jnp.bfloat16)
    shifts = jnp.dot(time_features[None, :], w_mod, preferred_element_type=jnp.float32)[0]
    return (shifts, sigma_next - sigma_now)


def own_state(key_heads, value_heads, cumulative):
    block_total = cumulative[:, -1]
    scaled = key_heads.astype(jnp.float32) * jnp.exp(block_total[:, None] - cumulative)[:, :, None]
    state_sum = jnp.einsum(
        "htd,hte->hde", scaled, value_heads.astype(jnp.float32), precision=lax.Precision.HIGHEST
    )
    return (block_total, state_sum)


def mix_block(query_heads, key_heads, value_heads, cumulative, labels, carried_state):
    factor = query_heads.shape[2] ** (-0.5)
    visible = labels[None, :] <= labels[:, None]
    decay = jnp.exp(jnp.minimum(cumulative[:, :, None] - cumulative[:, None, :], 0.0))
    weights = jnp.where(visible[None], decay, 0.0) * factor
    scores = jnp.einsum("hid,hjd->hij", query_heads, key_heads, preferred_element_type=jnp.float32)
    probs = (scores * weights).astype(jnp.bfloat16)
    inner_part = jnp.einsum("hij,hjd->hid", probs, value_heads, preferred_element_type=jnp.float32)
    carried = jnp.einsum(
        "hid,hde->hie",
        query_heads.astype(jnp.float32),
        carried_state,
        precision=lax.Precision.HIGHEST,
    )
    numerator = inner_part + carried * (jnp.exp(cumulative) * factor)[:, :, None]
    normed = numerator * lax.rsqrt(jnp.mean(numerator * numerator, axis=2, keepdims=True) + 1e-06)
    return normed.astype(jnp.bfloat16)


def layer_norm(hidden):
    centered = hidden - jnp.mean(hidden, axis=1, keepdims=True)
    variance = jnp.mean(centered * centered, axis=1, keepdims=True)
    return centered * lax.rsqrt(variance + 1e-06)


def by_collectives(
    latents, queries, keys, values, log_decay, block_ids, t_index, w_mod, w_out, w_up, w_down
):
    shifts, step_size = modulation_of(t_index, w_mod)
    width = latents.shape[1]
    head_count = log_decay.shape[0]
    token_count = log_decay.shape[1]
    head_size = queries.shape[1] // head_count

    def to_heads(rows_in):
        return rows_in.reshape(token_count, head_count, head_size).transpose(1, 0, 2)

    query_heads = to_heads(queries)
    key_heads = to_heads(keys)
    value_heads = to_heads(values)
    cumulative = jnp.cumsum(log_decay, axis=1)
    block_total, state_sum = own_state(key_heads, value_heads, cumulative)
    keep_factor = jnp.exp(block_total)[:, None, None]

    def relay(turn, incoming):
        return shifted(
            (keep_factor * incoming + state_sum).astype(jnp.bfloat16), "frame", 1
        ).astype(jnp.float32)

    carried_state = lax.fori_loop(0, lax.axis_size("frame") - 1, relay, jnp.zeros_like(state_sum))
    mixed = mix_block(query_heads, key_heads, value_heads, cumulative, block_ids, carried_state)
    mixed_rows = mixed.transpose(1, 0, 2).reshape(token_count, head_count * head_size)
    head_terms = jnp.dot(
        mixed_rows,
        lax.all_gather(w_out, "frame", axis=1, tiled=True),
        preferred_element_type=jnp.float32,
    )
    attention = lax.psum_scatter(
        head_terms.astype(jnp.bfloat16), "tensor", scatter_dimension=0, tiled=True
    ).astype(jnp.float32)
    hidden = latents.astype(jnp.float32) + shifts[3 * width :] * attention
    normed = (layer_norm(hidden) * (1.0 + shifts[width : 2 * width]) + shifts[:width]).astype(
        jnp.bfloat16
    )
    normed_all = lax.all_gather(normed, "tensor", axis=0, tiled=True)
    up_sums = jnp.dot(
        normed_all,
        lax.all_gather(w_up, "frame", axis=0, tiled=True),
        preferred_element_type=jnp.float32,
    )
    units = jax.nn.gelu(up_sums, approximate=True).astype(jnp.bfloat16)
    unit_terms = jnp.dot(
        units,
        lax.all_gather(w_down, "frame", axis=1, tiled=True),
        preferred_element_type=jnp.float32,
    )
    feed = lax.psum_scatter(
        unit_terms.astype(jnp.bfloat16), "tensor", scatter_dimension=0, tiled=True
    ).astype(jnp.float32)
    velocity = (hidden + shifts[2 * width : 3 * width] * feed).astype(jnp.bfloat16)
    advanced = (latents.astype(jnp.float32) + step_size * velocity.astype(jnp.float32)).astype(
        jnp.bfloat16
    )
    return (velocity, advanced)


MESH = pl.DeviceIdType.MESH


def at_most(count, value):
    return jnp.minimum(jnp.maximum(value, 0), count - 1)


def fused(
    sizes,
    q_ref, k_ref, v_ref, cum_ref, cum_col_ref, label_ref, label_col_ref, lat_ref, shift_ref, step_ref,
    w_out_ref, w_up_ref, w_down_ref,
    velocity_ref, advanced_ref,
    out_buf, up_buf, down_buf, state_out, state_in, mixed,
    first, first_in, spread, second, second_in, hidden, attended,
    own_sem, y_send, y_recv, core_send, core_recv, state_sems,
    first_send, first_recv, spread_send, spread_recv, second_send, second_recv,
):
    ranks, slabs, head_count, head_size, rows, tokens, halves = sizes
    z = lax.axis_index("tensor")
    f = lax.axis_index("frame")
    pool = lax.axis_index("pool")
    core = lax.rem(pool, 2)
    other_core = pool + 1 - 2 * core
    other_f = 1 - f
    factor = head_size ** (-0.5)

    barrier = pltpu.get_barrier_semaphore()
    pl.semaphore_signal(barrier, inc=1, device_id={"frame": other_f}, device_id_type=MESH)
    pl.semaphore_signal(barrier, inc=1, device_id={"pool": other_core}, device_id_type=MESH)

    @pl.when(z > 0)
    def _():
        pl.semaphore_signal(barrier, inc=1, device_id={"tensor": z - 1}, device_id_type=MESH)

    @pl.when(z < ranks - 1)
    def _():
        pl.semaphore_signal(barrier, inc=1, device_id={"tensor": z + 1}, device_id_type=MESH)

    sources = (w_out_ref, w_up_ref, w_down_ref)
    buffers = (out_buf, up_buf, down_buf)
    own_copies = [
        pltpu.make_async_copy(sources[i], buffers[i].at[f], own_sem.at[i]) for i in range(3)
    ]
    for copy in own_copies:
        copy.start()

    for h in range(head_count):
        cols = slice(h * head_size, (h + 1) * head_size)
        column = cum_col_ref[:, h : h + 1]
        total = cum_ref[h : h + 1, tokens - 1 : tokens]
        scaled = (k_ref[:, cols].astype(jnp.float32) * jnp.exp(total - column)).astype(jnp.bfloat16)
        state_out[h] = lax.dot_general(
            scaled, v_ref[:, cols], (((0,), (0,)), ((), ())), preferred_element_type=jnp.float32
        ).astype(jnp.bfloat16)

    links = 2 + (z > 0).astype(jnp.int32) + (z < ranks - 1).astype(jnp.int32)
    pl.semaphore_wait(barrier, links)

    state_copy = pltpu.make_async_remote_copy(
        src_ref=state_out, dst_ref=state_in, send_sem=state_sems.at[0], recv_sem=state_sems.at[1],
        device_id={"frame": other_f}, device_id_type=MESH,
    )

    @pl.when(f == 0)
    def _():
        state_copy.start()
        state_in[...] = jnp.zeros_like(state_in)

    def across(i, half):
        start, size = halves[i][half]
        part = pl.ds(start, size)
        return pltpu.make_async_remote_copy(
            src_ref=sources[i].at[part], dst_ref=buffers[i].at[f, part],
            send_sem=y_send.at[i], recv_sem=y_recv.at[i],
            device_id={"frame": other_f}, device_id_type=MESH,
        )

    def arrived(i, half):
        start, size = halves[i][half]
        part = pl.ds(start, size)
        return pltpu.make_async_remote_copy(
            src_ref=sources[i].at[part], dst_ref=buffers[i].at[other_f, part],
            send_sem=y_send.at[i], recv_sem=y_recv.at[i],
            device_id={"frame": other_f}, device_id_type=MESH,
        )

    def beside(i, half):
        start, size = halves[i][half]
        region = buffers[i].at[other_f, pl.ds(start, size)]
        return pltpu.make_async_remote_copy(
            src_ref=region, dst_ref=region, send_sem=core_send.at[i], recv_sem=core_recv.at[i],
            device_id={"pool": other_core}, device_id_type=MESH,
        )

    def each_half(act):
        for half in range(2):
            @pl.when(core == half)
            def _():
                act(half)

    for i in range(3):
        each_half(lambda half: across(i, half).start())

    def pass_on(i):
        def act(half):
            arrived(i, half).wait_recv()
            beside(i, half).start()
        each_half(act)

    def settle(i):
        own_copies[i].wait()
        each_half(lambda half: beside(i, 1 - half).wait_recv())

    visible = label_ref[...] <= label_col_ref[...]
    for h in range(head_count):
        cols = slice(h * head_size, (h + 1) * head_size)
        qh = q_ref[:, cols]
        scores = lax.dot_general(
            qh, k_ref[:, cols], (((1,), (1,)), ((), ())), preferred_element_type=jnp.float32
        )
        column = cum_col_ref[:, h : h + 1]
        decay = jnp.exp(jnp.minimum(column - cum_ref[h : h + 1, :], 0.0))
        probs = (scores * (jnp.where(visible, decay, 0.0) * factor)).astype(jnp.bfloat16)
        inner = jnp.dot(probs, v_ref[:, cols], preferred_element_type=jnp.float32)
        if h == 0:
            @pl.when(f > 0)
            def _():
                state_copy.wait_recv()
        carried = jnp.dot(qh, state_in[h], preferred_element_type=jnp.float32)
        numerator = inner + carried * (jnp.exp(column) * factor)
        power = jnp.mean(numerator * numerator, axis=1, keepdims=True)
        mixed[:, cols] = (numerator * lax.rsqrt(power + 1e-06)).astype(jnp.bfloat16)

    pass_on(0)
    settle(0)

    def rows_of(d):
        return pl.ds(pl.multiple_of(d * rows, rows), rows)

    def hop(buf, landing, send_sem, recv_sem, way, d, s):
        to = at_most(ranks, z + 1 - 2 * way)
        return pltpu.make_async_remote_copy(
            src_ref=buf.at[d, s], dst_ref=landing.at[way, d, s],
            send_sem=send_sem.at[d, s], recv_sem=recv_sem.at[way, d, s],
            device_id={"tensor": to}, device_id_type=MESH,
        )

    def hop1(way, d, s):
        return hop(first, first_in, first_send, first_recv, way, d, s)

    def hop2(way, d, s):
        return hop(second, second_in, second_send, second_recv, way, d, s)

    def has_upstream(way):
        return jnp.where(way == 0, z > 0, z < ranks - 1)

    def first_turn(turn, carry):
        step = turn // 2
        near = jnp.where(z < ranks // 2, 0, 1)
        way = lax.rem(turn + near, 2)
        d = jnp.where(way == 0, ranks - 1 - step, step)
        active = jnp.where(way == 0, d > z, d < z)

        @pl.when(active)
        def _():
            def slab(s, c):
                part = jnp.dot(mixed[rows_of(d), :], out_buf[s], preferred_element_type=jnp.float32)
                first[d, s] = part.astype(jnp.bfloat16)

                @pl.when(has_upstream(way))
                def _():
                    hop1(way, d, s).wait_recv()
                    first[d, s] = (
                        first[d, s].astype(jnp.float32) + first_in[way, d, s].astype(jnp.float32)
                    ).astype(jnp.bfloat16)

                hop1(way, d, s).start()
                return c

            lax.fori_loop(0, slabs, slab, 0)

        return carry

    lax.fori_loop(0, 2 * (ranks - 1), first_turn, 0)

    def own_slab(s, c):
        part = jnp.dot(mixed[rows_of(z), :], out_buf[s], preferred_element_type=jnp.float32)
        attended[s] = part.astype(jnp.bfloat16).astype(jnp.float32)
        return c

    lax.fori_loop(0, slabs, own_slab, 0)
    pass_on(1)

    def gather_sums(hop_of, landing, target):
        for way in range(2):
            @pl.when(has_upstream(way))
            def _():
                for s in range(slabs):
                    hop_of(way, z, s).wait_recv()
                    target[s] += landing[way, z, s].astype(jnp.float32)

    gather_sums(hop1, first_in, attended)

    total = jnp.zeros((rows, 1), jnp.float32)
    for s in range(slabs):
        value = lat_ref[s].astype(jnp.float32) + shift_ref[3, s] * attended[s]
        hidden[s] = value
        total += jnp.sum(value, axis=1, keepdims=True)
    width = slabs * hidden.shape[2]
    mean = total / width
    squares = jnp.zeros((rows, 1), jnp.float32)
    for s in range(slabs):
        centered = hidden[s] - mean
        squares += jnp.sum(centered * centered, axis=1, keepdims=True)
    inverse = lax.rsqrt(squares / width + 1e-06)
    for s in range(slabs):
        spread[z, s] = (
            (hidden[s] - mean) * inverse * (1.0 + shift_ref[1, s]) + shift_ref[0, s]
        ).astype(jnp.bfloat16)

    def relay(way, c, s):
        to = at_most(ranks, z + 1 - 2 * way)
        return pltpu.make_async_remote_copy(
            src_ref=spread.at[c, s], dst_ref=spread.at[c, s],
            send_sem=spread_send.at[way, c, s], recv_sem=spread_recv.at[c, s],
            device_id={"tensor": to}, device_id_type=MESH,
        )

    def has_downstream(way):
        return jnp.where(way == 0, z < ranks - 1, z > 0)

    for way in range(2):
        @pl.when(has_downstream(way))
        def _():
            for s in range(slabs):
                relay(way, z, s).start()

    settle(1)

    def tick(k, carry):
        def arrival(way, c0):
            c = jnp.where(way == 0, z - k, z + k)
            valid = (c >= 0) & (c < ranks) & ((k > 0) | (way == 0))

            @pl.when(valid)
            def _():
                @pl.when(k > 0)
                def _():
                    for s in range(slabs):
                        relay(way, c, s).wait_recv()

                        @pl.when(has_downstream(way))
                        def _():
                            relay(way, c, s).start()

                acc = jnp.dot(spread[c, 0], up_buf[0], preferred_element_type=jnp.float32)
                for s in range(1, slabs):
                    acc += jnp.dot(spread[c, s], up_buf[s], preferred_element_type=jnp.float32)
                units = jax.nn.gelu(acc, approximate=True).astype(jnp.bfloat16)

                @pl.when(k == 0)
                def _():
                    pass_on(2)
                    settle(2)

                for s in range(slabs):
                    second[c, s] = jnp.dot(
                        units, down_buf[s], preferred_element_type=jnp.float32
                    ).astype(jnp.bfloat16)

            return c0

        @pl.when(k < ranks)
        def _():
            lax.fori_loop(0, 2, arrival, 0)

        def sending(way, c0):
            place = jnp.where(way == 0, z, ranks - 1 - z)
            ahead = k - place
            d = jnp.where(way == 0, ahead, ranks - 1 - ahead)

            @pl.when((ahead > place) & (ahead < ranks))
            def _():
                def slab(s, c1):
                    @pl.when(has_upstream(way))
                    def _():
                        hop2(way, d, s).wait_recv()
                        second[d, s] = (
                            second[d, s].astype(jnp.float32) + second_in[way, d, s].astype(jnp.float32)
                        ).astype(jnp.bfloat16)

                    hop2(way, d, s).start()
                    return c1

                lax.fori_loop(0, slabs, slab, 0)

            return c0

        lax.fori_loop(0, 2, sending, 0)
        return carry

    lax.fori_loop(0, 2 * ranks - 2, tick, 0)

    for s in range(slabs):
        attended[s] = second[z, s].astype(jnp.float32)
    gather_sums(hop2, second_in, attended)
    step = step_ref[...]
    for s in range(slabs):
        velocity = (hidden[s] + shift_ref[2, s] * attended[s]).astype(jnp.bfloat16)
        velocity_ref[s] = velocity
        advanced_ref[s] = (
            lat_ref[s].astype(jnp.float32) + step * velocity.astype(jnp.float32)
        ).astype(jnp.bfloat16)

    @pl.when(f == 0)
    def _():
        state_copy.wait_send()

    for i in range(3):
        each_half(lambda half: across(i, half).wait_send())
        each_half(lambda half: beside(i, half).wait_send())

    def drain(d, carry):
        def slab(s, c):
            @pl.when(d != z)
            def _():
                way = jnp.where(d > z, 0, 1)
                hop1(way, d, s).wait_send()
                hop2(way, d, s).wait_send()

            def direction(way, c1):
                came = jnp.where(way == 0, d <= z, d >= z)

                @pl.when(came & has_downstream(way))
                def _():
                    relay(way, d, s).wait_send()

                return c1

            lax.fori_loop(0, 2, direction, 0)
            return c

        lax.fori_loop(0, slabs, slab, 0)
        return carry

    lax.fori_loop(0, ranks, drain, 0)


def fits(latents, queries, log_decay, w_out, w_up, w_down):
    frames, ranks, pools = (lax.axis_size(a) for a in ("frame", "tensor", "pool"))
    rows, tokens = latents.shape[0], queries.shape[0]
    return (
        frames == 2
        and pools % 2 == 0
        and rows * ranks == tokens
        and rows % 16 == 0
        and all(w.shape[0] % 16 == 0 and w.shape[0] >= 32 for w in (w_out, w_up, w_down))
        and w_up.shape[0] == w_out.shape[1] == w_down.shape[1]
        and queries.shape[1] // log_decay.shape[0] % 16 == 0
    )


def on_device(
    latents, queries, keys, values, log_decay, block_ids, t_index, w_mod, w_out, w_up, w_down
):
    if not fits(latents, queries, log_decay, w_out, w_up, w_down):
        return by_collectives(
            latents, queries, keys, values, log_decay, block_ids, t_index, w_mod, w_out, w_up, w_down
        )
    ranks, slabs = lax.axis_size("tensor"), lax.axis_size("frame")
    rows, width = latents.shape
    piece = width // slabs
    tokens, features = queries.shape
    head_count = log_decay.shape[0]
    head_size = features // head_count
    shifts, step_size = modulation_of(t_index, w_mod)
    cumulative = jnp.cumsum(log_decay, axis=1)

    def split(count):
        front = -(-count // 32) * 16
        return ((0, front), (front, count - front))

    halves = tuple(split(w.shape[0]) for w in (w_out, w_up, w_down))
    sizes = (ranks, slabs, head_count, head_size, rows, tokens, halves)
    block = (ranks, slabs, rows, piece)
    vmem = pl.BlockSpec(memory_space=pltpu.VMEM)
    anywhere = pl.BlockSpec(memory_space=pl.ANY)
    dma = pltpu.SemaphoreType.DMA
    velocity, advanced = pl.pallas_call(
        functools.partial(fused, sizes),
        out_shape=[jax.ShapeDtypeStruct((slabs, rows, piece), jnp.bfloat16)] * 2,
        in_specs=[vmem] * 10 + [anywhere] * 3,
        out_specs=[vmem] * 2,
        scratch_shapes=[
            pltpu.VMEM((slabs,) + w_out.shape, jnp.bfloat16),
            pltpu.VMEM((slabs,) + w_up.shape, jnp.bfloat16),
            pltpu.VMEM((slabs,) + w_down.shape, jnp.bfloat16),
            pltpu.VMEM((head_count, head_size, head_size), jnp.bfloat16),
            pltpu.VMEM((head_count, head_size, head_size), jnp.bfloat16),
            pltpu.VMEM((tokens, features), jnp.bfloat16),
            pltpu.VMEM(block, jnp.bfloat16),
            pltpu.VMEM((2,) + block, jnp.bfloat16),
            pltpu.VMEM(block, jnp.bfloat16),
            pltpu.VMEM(block, jnp.bfloat16),
            pltpu.VMEM((2,) + block, jnp.bfloat16),
            pltpu.VMEM((slabs, rows, piece), jnp.float32),
            pltpu.VMEM((slabs, rows, piece), jnp.float32),
            dma((3,)), dma((3,)), dma((3,)), dma((3,)), dma((3,)), dma((2,)),
            dma((ranks, slabs)), dma((2, ranks, slabs)),
            dma((2, ranks, slabs)), dma((ranks, slabs)),
            dma((ranks, slabs)), dma((2, ranks, slabs)),
        ],
        compiler_params=pltpu.CompilerParams(
            collective_id=0, has_side_effects=True, vmem_limit_bytes=56 * 1024 * 1024
        ),
        name="sublayers",
    )(
        queries, keys, values, cumulative, cumulative.T, block_ids[None, :], block_ids[:, None],
        latents.reshape(rows, slabs, piece).transpose(1, 0, 2),
        shifts.reshape(4, slabs, 1, piece), step_size.reshape(1, 1),
        w_out, w_up, w_down,
    )

    def whole_rows(blocks):
        return blocks.transpose(1, 0, 2).reshape(rows, width)

    return (whole_rows(velocity), whole_rows(advanced))


def solution(mesh):
    return jax.shard_map(
        on_device,
        mesh=mesh,
        in_specs=(
            P(("pool", "frame", "tensor"), None),
            P(("pool", "frame"), "tensor"),
            P(("pool", "frame"), "tensor"),
            P(("pool", "frame"), "tensor"),
            P("tensor", ("pool", "frame")),
            P(("pool", "frame")),
            P("pool"),
            P(),
            P("tensor", "frame"),
            P("frame", "tensor"),
            P("tensor", "frame"),
        ),
        out_specs=(P(("pool", "frame", "tensor"), None), P(("pool", "frame", "tensor"), None)),
        check_vma=False,
    )
```

```python
import functools
import math

import jax
import jax.numpy as jnp
from jax import lax
from jax.experimental import pallas as pl
from jax.experimental.pallas import tpu as pltpu
from jax.sharding import PartitionSpec as P

STEPS = 50


def shifted(block, axis, distance):
    devices = range(lax.axis_size(axis))
    route = [(i - distance, i) for i in devices if i - distance in devices]
    return lax.ppermute(block, axis, route)


def time_embedding(t_index, w_mod):
    fraction = 1.0 - t_index[0].astype(jnp.float32) / STEPS
    following = fraction - 1.0 / STEPS
    sigma_now = 3.0 * fraction / (1.0 + 2.0 * fraction)
    sigma_next = 3.0 * following / (1.0 + 2.0 * following)
    half_width = w_mod.shape[0] // 2
    frequency = jnp.exp(
        -math.log(10000.0) * jnp.arange(half_width).astype(jnp.float32) / half_width
    )
    angles = 1000.0 * sigma_now * frequency
    embedding = jnp.concatenate([jnp.cos(angles), jnp.sin(angles)])
    return (jax.nn.silu(embedding).astype(jnp.bfloat16), sigma_next - sigma_now)


def modulation_of(t_index, w_mod):
    time_features, step_size = time_embedding(t_index, w_mod)
    shifts = jnp.dot(time_features[None, :], w_mod, preferred_element_type=jnp.float32)[0]
    return (shifts, step_size)


def own_state(key_heads, value_heads, cumulative):
    block_total = cumulative[:, -1]
    scaled = key_heads.astype(jnp.float32) * jnp.exp(block_total[:, None] - cumulative)[:, :, None]
    state_sum = jnp.einsum(
        "htd,hte->hde", scaled, value_heads.astype(jnp.float32), precision=lax.Precision.HIGHEST
    )
    return (block_total, state_sum)


def mix_block(query_heads, key_heads, value_heads, cumulative, labels, carried_state):
    factor = query_heads.shape[2] ** (-0.5)
    visible = labels[None, :] <= labels[:, None]
    decay = jnp.exp(jnp.minimum(cumulative[:, :, None] - cumulative[:, None, :], 0.0))
    weights = jnp.where(visible[None], decay, 0.0) * factor
    scores = jnp.einsum("hid,hjd->hij", query_heads, key_heads, preferred_element_type=jnp.float32)
    probs = (scores * weights).astype(jnp.bfloat16)
    inner_part = jnp.einsum("hij,hjd->hid", probs, value_heads, preferred_element_type=jnp.float32)
    carried = jnp.einsum(
        "hid,hde->hie",
        query_heads.astype(jnp.float32),
        carried_state,
        precision=lax.Precision.HIGHEST,
    )
    numerator = inner_part + carried * (jnp.exp(cumulative) * factor)[:, :, None]
    normed = numerator * lax.rsqrt(jnp.mean(numerator * numerator, axis=2, keepdims=True) + 1e-06)
    return normed.astype(jnp.bfloat16)


def layer_norm(hidden):
    centered = hidden - jnp.mean(hidden, axis=1, keepdims=True)
    variance = jnp.mean(centered * centered, axis=1, keepdims=True)
    return centered * lax.rsqrt(variance + 1e-06)


def by_collectives(
    latents, queries, keys, values, log_decay, block_ids, t_index, w_mod, w_out, w_up, w_down
):
    shifts, step_size = modulation_of(t_index, w_mod)
    width = latents.shape[1]
    head_count = log_decay.shape[0]
    token_count = log_decay.shape[1]
    head_size = queries.shape[1] // head_count

    def to_heads(rows_in):
        return rows_in.reshape(token_count, head_count, head_size).transpose(1, 0, 2)

    query_heads = to_heads(queries)
    key_heads = to_heads(keys)
    value_heads = to_heads(values)
    cumulative = jnp.cumsum(log_decay, axis=1)
    block_total, state_sum = own_state(key_heads, value_heads, cumulative)
    keep_factor = jnp.exp(block_total)[:, None, None]

    def relay(turn, incoming):
        return shifted(
            (keep_factor * incoming + state_sum).astype(jnp.bfloat16), "frame", 1
        ).astype(jnp.float32)

    carried_state = lax.fori_loop(0, lax.axis_size("frame") - 1, relay, jnp.zeros_like(state_sum))
    mixed = mix_block(query_heads, key_heads, value_heads, cumulative, block_ids, carried_state)
    mixed_rows = mixed.transpose(1, 0, 2).reshape(token_count, head_count * head_size)
    head_terms = jnp.dot(
        mixed_rows,
        lax.all_gather(w_out, "frame", axis=1, tiled=True),
        preferred_element_type=jnp.float32,
    )
    attention = lax.psum_scatter(
        head_terms.astype(jnp.bfloat16), "tensor", scatter_dimension=0, tiled=True
    ).astype(jnp.float32)
    hidden = latents.astype(jnp.float32) + shifts[3 * width :] * attention
    normed = (layer_norm(hidden) * (1.0 + shifts[width : 2 * width]) + shifts[:width]).astype(
        jnp.bfloat16
    )
    normed_all = lax.all_gather(normed, "tensor", axis=0, tiled=True)
    up_sums = jnp.dot(
        normed_all,
        lax.all_gather(w_up, "frame", axis=0, tiled=True),
        preferred_element_type=jnp.float32,
    )
    units = jax.nn.gelu(up_sums, approximate=True).astype(jnp.bfloat16)
    unit_terms = jnp.dot(
        units,
        lax.all_gather(w_down, "frame", axis=1, tiled=True),
        preferred_element_type=jnp.float32,
    )
    feed = lax.psum_scatter(
        unit_terms.astype(jnp.bfloat16), "tensor", scatter_dimension=0, tiled=True
    ).astype(jnp.float32)
    velocity = (hidden + shifts[2 * width : 3 * width] * feed).astype(jnp.bfloat16)
    advanced = (latents.astype(jnp.float32) + step_size * velocity.astype(jnp.float32)).astype(
        jnp.bfloat16
    )
    return (velocity, advanced)


MESH = pl.DeviceIdType.MESH


def at_most(count, value):
    return jnp.minimum(jnp.maximum(value, 0), count - 1)


def fused(
    sizes,
    q_ref, k_ref, v_ref, decay_ref, label_ref, lat_ref, feature_ref, step_ref,
    w_out_ref, w_up_ref, w_down_ref, w_mod_ref,
    velocity_ref, advanced_ref,
    out_buf, up_buf, down_buf, mod_buf, state_out, state_in, mixed,
    first, first_in, spread, second, second_in, hidden, attended, units_own, columns, shift_rows,
    own_sem, y_send, y_recv, x_send, x_recv, core_send, core_recv, state_sems,
    first_send, first_recv, spread_send, spread_recv, second_send, second_recv,
):
    ranks, slabs, head_count, head_size, rows, tokens, quarters = sizes
    z = lax.axis_index("tensor")
    f = lax.axis_index("frame")
    pool = lax.axis_index("pool")
    core = lax.rem(pool, 2)
    other_core = pool + 1 - 2 * core
    other_chip = lax.rem(pool + 2, 4)
    other_f = 1 - f
    factor = head_size ** (-0.5)

    barrier = pltpu.get_barrier_semaphore()
    pl.semaphore_signal(barrier, inc=1, device_id={"frame": other_f}, device_id_type=MESH)
    pl.semaphore_signal(barrier, inc=1, device_id={"pool": other_core}, device_id_type=MESH)
    pl.semaphore_signal(barrier, inc=1, device_id={"pool": other_chip}, device_id_type=MESH)

    @pl.when(z > 0)
    def _():
        pl.semaphore_signal(barrier, inc=1, device_id={"tensor": z - 1}, device_id_type=MESH)

    @pl.when(z < ranks - 1)
    def _():
        pl.semaphore_signal(barrier, inc=1, device_id={"tensor": z + 1}, device_id_type=MESH)

    sources = (w_out_ref, w_up_ref, w_down_ref)
    buffers = (out_buf, up_buf, down_buf)
    own_copies = [
        pltpu.make_async_copy(sources[i], buffers[i].at[f], own_sem.at[i]) for i in range(3)
    ]
    for copy in own_copies:
        copy.start()
    mod_copy = pltpu.make_async_copy(w_mod_ref, mod_buf, own_sem.at[3])
    mod_copy.start()

    earlier = (
        lax.broadcasted_iota(jnp.int32, (tokens, tokens), 0)
        <= lax.broadcasted_iota(jnp.int32, (tokens, tokens), 1)
    ).astype(jnp.float32).astype(jnp.bfloat16)
    rest = decay_ref[...]
    cum = jnp.zeros_like(rest)
    for _ in range(3):
        leading = rest.astype(jnp.bfloat16)
        rest = rest - leading.astype(jnp.float32)
        cum += jnp.dot(leading, earlier, preferred_element_type=jnp.float32)
    columns[...] = jnp.zeros_like(columns)
    columns[0:head_count, :] = cum
    columns[head_count : head_count + 1, :] = label_ref[...].astype(jnp.float32)
    cum_col = columns[...].T

    for h in range(head_count):
        part = slice(h * head_size, (h + 1) * head_size)
        row = cum[h : h + 1, :]
        total = row[:, tokens - 1 : tokens]
        scaled = (k_ref[part, :].astype(jnp.float32) * jnp.exp(total - row)).astype(jnp.bfloat16)
        state_out[h] = lax.dot_general(
            v_ref[part, :], scaled, (((1,), (1,)), ((), ())), preferred_element_type=jnp.float32
        ).astype(jnp.bfloat16)

    links = 3 + (z > 0).astype(jnp.int32) + (z < ranks - 1).astype(jnp.int32)
    pl.semaphore_wait(barrier, links)

    state_copy = pltpu.make_async_remote_copy(
        src_ref=state_out, dst_ref=state_in, send_sem=state_sems.at[0], recv_sem=state_sems.at[1],
        device_id={"frame": other_f}, device_id_type=MESH,
    )

    @pl.when(f == 0)
    def _():
        state_copy.start()
        state_in[...] = jnp.zeros_like(state_in)

    def across(i, quarter):
        part = pl.ds(*quarters[i][quarter])
        return pltpu.make_async_remote_copy(
            src_ref=sources[i].at[part], dst_ref=buffers[i].at[f, part],
            send_sem=y_send.at[i], recv_sem=y_recv.at[i],
            device_id={"frame": other_f}, device_id_type=MESH,
        )

    def arrived(i, quarter):
        part = pl.ds(*quarters[i][quarter])
        return pltpu.make_async_remote_copy(
            src_ref=sources[i].at[part], dst_ref=buffers[i].at[other_f, part],
            send_sem=y_send.at[i], recv_sem=y_recv.at[i],
            device_id={"frame": other_f}, device_id_type=MESH,
        )

    def region(i, quarter):
        return buffers[i].at[other_f, pl.ds(*quarters[i][quarter])]

    def to_chip(i, quarter):
        return pltpu.make_async_remote_copy(
            src_ref=region(i, quarter), dst_ref=region(i, quarter),
            send_sem=x_send.at[i], recv_sem=x_recv.at[i],
            device_id={"pool": other_chip}, device_id_type=MESH,
        )

    def to_core(i, quarter, turn):
        return pltpu.make_async_remote_copy(
            src_ref=region(i, quarter), dst_ref=region(i, quarter),
            send_sem=core_send.at[i, turn], recv_sem=core_recv.at[i, turn],
            device_id={"pool": other_core}, device_id_type=MESH,
        )

    def each_quarter(act):
        for quarter in range(4):
            @pl.when(pool == quarter)
            def _():
                act(quarter)

    for i in range(3):
        each_quarter(lambda quarter: across(i, quarter).start())

    def pass_on(i):
        def act(quarter):
            arrived(i, quarter).wait_recv()
            to_chip(i, quarter).start()
            to_core(i, quarter, 0).start()
        each_quarter(act)

    def pass_round(i):
        def act(quarter):
            opposite = (quarter + 2) % 4
            to_chip(i, opposite).wait_recv()
            to_core(i, opposite, 1).start()
        each_quarter(act)

    def settle(i):
        def act(quarter):
            to_core(i, quarter ^ 1, 0).wait_recv()
            to_core(i, (quarter ^ 1) ^ 2, 1).wait_recv()
        own_copies[i].wait()
        each_quarter(act)

    visible = cum_col[:, head_count : head_count + 1] <= columns[head_count : head_count + 1, :]
    for h in range(head_count):
        part = slice(h * head_size, (h + 1) * head_size)
        qh = q_ref[part, :]
        scores = lax.dot_general(
            k_ref[part, :], qh, (((0,), (0,)), ((), ())), preferred_element_type=jnp.float32
        )
        row = cum[h : h + 1, :]
        decay = jnp.exp(jnp.minimum(row - cum_col[:, h : h + 1], 0.0))
        probs = (scores * (jnp.where(visible, decay, 0.0) * factor)).astype(jnp.bfloat16)
        inner = jnp.dot(v_ref[part, :], probs, preferred_element_type=jnp.float32)
        if h == 0:
            @pl.when(f > 0)
            def _():
                state_copy.wait_recv()
        carried = jnp.dot(state_in[h], qh, preferred_element_type=jnp.float32)
        numerator = inner + carried * (jnp.exp(row) * factor)
        power = jnp.mean(numerator * numerator, axis=0, keepdims=True)
        mixed[:, part] = (numerator * lax.rsqrt(power + 1e-06)).T.astype(jnp.bfloat16)

    pass_on(0)
    pass_round(0)
    settle(0)

    def rows_of(d):
        return pl.ds(pl.multiple_of(d * rows, rows), rows)

    def hop(buf, landing, send_sem, recv_sem, way, d, s):
        to = at_most(ranks, z + 1 - 2 * way)
        return pltpu.make_async_remote_copy(
            src_ref=buf.at[d, s], dst_ref=landing.at[way, d, s],
            send_sem=send_sem.at[d, s], recv_sem=recv_sem.at[way, d, s],
            device_id={"tensor": to}, device_id_type=MESH,
        )

    def hop1(way, d, s):
        return hop(first, first_in, first_send, first_recv, way, d, s)

    def hop2(way, d, s):
        return hop(second, second_in, second_send, second_recv, way, d, s)

    def has_upstream(way):
        return jnp.where(way == 0, z > 0, z < ranks - 1)

    def first_turn(turn, carry):
        step = turn // 2
        near = jnp.where(z < ranks // 2, 0, 1)
        way = lax.rem(turn + near, 2)
        d = jnp.where(way == 0, ranks - 1 - step, step)
        active = jnp.where(way == 0, d > z, d < z)

        @pl.when(active)
        def _():
            def slab(s, c):
                part = jnp.dot(mixed[rows_of(d), :], out_buf[s], preferred_element_type=jnp.float32)
                first[d, s] = part.astype(jnp.bfloat16)

                @pl.when(has_upstream(way))
                def _():
                    hop1(way, d, s).wait_recv()
                    first[d, s] = (
                        first[d, s].astype(jnp.float32) + first_in[way, d, s].astype(jnp.float32)
                    ).astype(jnp.bfloat16)

                hop1(way, d, s).start()
                return c

            lax.fori_loop(0, slabs, slab, 0)

        return carry

    lax.fori_loop(0, 2 * (ranks - 1), first_turn, 0)

    def own_slab(s, c):
        part = jnp.dot(mixed[rows_of(z), :], out_buf[s], preferred_element_type=jnp.float32)
        attended[s] = part.astype(jnp.bfloat16).astype(jnp.float32)
        return c

    lax.fori_loop(0, slabs, own_slab, 0)
    pass_on(1)

    mod_copy.wait()
    shift_rows[...] = jnp.dot(feature_ref[...], mod_buf[...], preferred_element_type=jnp.float32)
    piece = hidden.shape[2]

    def shift(kind, s):
        start = (kind * slabs + s) * piece
        return shift_rows[0:1, start : start + piece]

    def lat(s):
        return lat_ref[s * piece : (s + 1) * piece, :].astype(jnp.float32).T

    pass_round(1)

    def gather_sums(hop_of, landing, target):
        for way in range(2):
            @pl.when(has_upstream(way))
            def _():
                for s in range(slabs):
                    hop_of(way, z, s).wait_recv()
                    target[s] += landing[way, z, s].astype(jnp.float32)

    gather_sums(hop1, first_in, attended)

    total = jnp.zeros((rows, 1), jnp.float32)
    for s in range(slabs):
        value = lat(s) + shift(3, s) * attended[s]
        hidden[s] = value
        total += jnp.sum(value, axis=1, keepdims=True)
    width = slabs * hidden.shape[2]
    mean = total / width
    squares = jnp.zeros((rows, 1), jnp.float32)
    for s in range(slabs):
        centered = hidden[s] - mean
        squares += jnp.sum(centered * centered, axis=1, keepdims=True)
    inverse = lax.rsqrt(squares / width + 1e-06)
    for s in range(slabs):
        spread[z, s] = (
            (hidden[s] - mean) * inverse * (1.0 + shift(1, s)) + shift(0, s)
        ).astype(jnp.bfloat16)

    def relay(way, c, s):
        to = at_most(ranks, z + 1 - 2 * way)
        return pltpu.make_async_remote_copy(
            src_ref=spread.at[c, s], dst_ref=spread.at[c, s],
            send_sem=spread_send.at[way, c, s], recv_sem=spread_recv.at[c, s],
            device_id={"tensor": to}, device_id_type=MESH,
        )

    def has_downstream(way):
        return jnp.where(way == 0, z < ranks - 1, z > 0)

    for way in range(2):
        @pl.when(has_downstream(way))
        def _():
            for s in range(slabs):
                relay(way, z, s).start()

    settle(1)

    def up_side(c):
        acc = jnp.dot(spread[c, 0], up_buf[0], preferred_element_type=jnp.float32)
        for s in range(1, slabs):
            acc += jnp.dot(spread[c, s], up_buf[s], preferred_element_type=jnp.float32)
        return jax.nn.gelu(acc, approximate=True).astype(jnp.bfloat16)

    units_own[...] = up_side(z)
    pass_on(2)
    pass_round(2)

    def tick(k, carry):
        def chunk_of(way):
            return jnp.where(way == 0, z - k, z + k)

        def arrival(way, c0):
            c = chunk_of(way)

            @pl.when((c >= 0) & (c < ranks))
            def _():
                for s in range(slabs):
                    relay(way, c, s).wait_recv()

                    @pl.when(has_downstream(way))
                    def _():
                        relay(way, c, s).start()

            return c0

        def work(way, c0):
            c = chunk_of(way)

            @pl.when((c >= 0) & (c < ranks))
            def _():
                units = up_side(c)

                @pl.when((k == 1) & ((way == 0) | (z == 0)))
                def _():
                    settle(2)

                for s in range(slabs):
                    second[c, s] = jnp.dot(
                        units, down_buf[s], preferred_element_type=jnp.float32
                    ).astype(jnp.bfloat16)

            return c0

        @pl.when(k < ranks)
        def _():
            lax.fori_loop(0, 2, arrival, 0)
            lax.fori_loop(0, 2, work, 0)

        def sending(way, c0):
            place = jnp.where(way == 0, z, ranks - 1 - z)
            ahead = k - place
            d = jnp.where(way == 0, ahead, ranks - 1 - ahead)

            @pl.when((ahead > place) & (ahead < ranks))
            def _():
                def slab(s, c1):
                    @pl.when(has_upstream(way))
                    def _():
                        hop2(way, d, s).wait_recv()
                        second[d, s] = (
                            second[d, s].astype(jnp.float32) + second_in[way, d, s].astype(jnp.float32)
                        ).astype(jnp.bfloat16)

                    hop2(way, d, s).start()
                    return c1

                lax.fori_loop(0, slabs, slab, 0)

            return c0

        lax.fori_loop(0, 2, sending, 0)
        return carry

    lax.fori_loop(1, 2 * ranks - 2, tick, 0)

    for s in range(slabs):
        attended[s] = (
            jnp.dot(units_own[...], down_buf[s], preferred_element_type=jnp.float32)
            .astype(jnp.bfloat16)
            .astype(jnp.float32)
        )
    gather_sums(hop2, second_in, attended)
    step = step_ref[...]
    for s in range(slabs):
        velocity = (hidden[s] + shift(2, s) * attended[s]).astype(jnp.bfloat16).astype(jnp.float32)
        part = slice(s * piece, (s + 1) * piece)
        velocity = velocity.T
        velocity_ref[part, :] = velocity.astype(jnp.bfloat16)
        advanced_ref[part, :] = (
            lat_ref[part, :].astype(jnp.float32) + step * velocity
        ).astype(jnp.bfloat16)

    @pl.when(f == 0)
    def _():
        state_copy.wait_send()

    for i in range(3):
        def left(quarter):
            across(i, quarter).wait_send()
            to_chip(i, quarter).wait_send()
            to_core(i, quarter, 0).wait_send()
            to_core(i, (quarter + 2) % 4, 1).wait_send()
        each_quarter(left)

    def drain(d, carry):
        def slab(s, c):
            @pl.when(d != z)
            def _():
                way = jnp.where(d > z, 0, 1)
                hop1(way, d, s).wait_send()
                hop2(way, d, s).wait_send()

            def direction(way, c1):
                came = jnp.where(way == 0, d <= z, d >= z)

                @pl.when(came & has_downstream(way))
                def _():
                    relay(way, d, s).wait_send()

                return c1

            lax.fori_loop(0, 2, direction, 0)
            return c

        lax.fori_loop(0, slabs, slab, 0)
        return carry

    lax.fori_loop(0, ranks, drain, 0)


def fits(latents, queries, log_decay, w_out, w_up, w_down):
    frames, ranks, pools = (lax.axis_size(a) for a in ("frame", "tensor", "pool"))
    rows, tokens = latents.shape[0], queries.shape[0]
    return (
        frames == 2
        and pools == 4
        and ranks > 1
        and rows % 128 == 0
        and latents.shape[1] % (16 * frames) == 0
        and log_decay.shape[0] < 8
        and rows * ranks == tokens
        and rows % 16 == 0
        and all(w.shape[0] % 16 == 0 and w.shape[0] >= 64 for w in (w_out, w_up, w_down))
        and w_up.shape[0] == w_out.shape[1] == w_down.shape[1]
        and queries.shape[1] // log_decay.shape[0] % 16 == 0
    )


def on_device(
    latents, queries, keys, values, log_decay, block_ids, t_index, w_mod, w_out, w_up, w_down
):
    if not fits(latents, queries, log_decay, w_out, w_up, w_down):
        return by_collectives(
            latents, queries, keys, values, log_decay, block_ids, t_index, w_mod, w_out, w_up, w_down
        )
    ranks, slabs = lax.axis_size("tensor"), lax.axis_size("frame")
    rows, width = latents.shape
    piece = width // slabs
    tokens, features = queries.shape
    head_count = log_decay.shape[0]
    head_size = features // head_count
    time_features, step_size = time_embedding(t_index, w_mod)

    def split(count):
        edges = [count // 16 * i // 4 * 16 for i in range(5)]
        return tuple((edges[i], edges[i + 1] - edges[i]) for i in range(4))

    quarters = tuple(split(w.shape[0]) for w in (w_out, w_up, w_down))
    sizes = (ranks, slabs, head_count, head_size, rows, tokens, quarters)
    block = (ranks, slabs, rows, piece)
    vmem = pl.BlockSpec(memory_space=pltpu.VMEM)
    anywhere = pl.BlockSpec(memory_space=pl.ANY)
    dma = pltpu.SemaphoreType.DMA
    velocity, advanced = pl.pallas_call(
        functools.partial(fused, sizes),
        out_shape=[jax.ShapeDtypeStruct((width, rows), jnp.bfloat16)] * 2,
        in_specs=[vmem] * 8 + [anywhere] * 4,
        out_specs=[vmem] * 2,
        scratch_shapes=[
            pltpu.VMEM((slabs,) + w_out.shape, jnp.bfloat16),
            pltpu.VMEM((slabs,) + w_up.shape, jnp.bfloat16),
            pltpu.VMEM((slabs,) + w_down.shape, jnp.bfloat16),
            pltpu.VMEM(w_mod.shape, jnp.bfloat16),
            pltpu.VMEM((head_count, head_size, head_size), jnp.bfloat16),
            pltpu.VMEM((head_count, head_size, head_size), jnp.bfloat16),
            pltpu.VMEM((tokens, features), jnp.bfloat16),
            pltpu.VMEM(block, jnp.bfloat16),
            pltpu.VMEM((2,) + block, jnp.bfloat16),
            pltpu.VMEM(block, jnp.bfloat16),
            pltpu.VMEM(block, jnp.bfloat16),
            pltpu.VMEM((2,) + block, jnp.bfloat16),
            pltpu.VMEM((slabs, rows, piece), jnp.float32),
            pltpu.VMEM((slabs, rows, piece), jnp.float32),
            pltpu.VMEM((rows, w_up.shape[1]), jnp.bfloat16),
            pltpu.VMEM((8, tokens), jnp.float32),
            pltpu.VMEM((8, w_mod.shape[1]), jnp.float32),
            dma((4,)), dma((3,)), dma((3,)), dma((3,)), dma((3,)), dma((3, 2)), dma((3, 2)), dma((2,)),
            dma((ranks, slabs)), dma((2, ranks, slabs)),
            dma((2, ranks, slabs)), dma((ranks, slabs)),
            dma((ranks, slabs)), dma((2, ranks, slabs)),
        ],
        compiler_params=pltpu.CompilerParams(
            collective_id=0, has_side_effects=True, vmem_limit_bytes=56 * 1024 * 1024
        ),
        name="sublayers",
    )(
        queries.T, keys.T, values.T, log_decay, block_ids[None, :], latents.T,
        jnp.broadcast_to(time_features, (8, time_features.shape[0])), step_size.reshape(1, 1),
        w_out, w_up, w_down, w_mod,
    )
    return (velocity.T, advanced.T)


def solution(mesh):
    return jax.shard_map(
        on_device,
        mesh=mesh,
        in_specs=(
            P(("pool", "frame", "tensor"), None),
            P(("pool", "frame"), "tensor"),
            P(("pool", "frame"), "tensor"),
            P(("pool", "frame"), "tensor"),
            P("tensor", ("pool", "frame")),
            P(("pool", "frame")),
            P("pool"),
            P(),
            P("tensor", "frame"),
            P("frame", "tensor"),
            P("tensor", "frame"),
        ),
        out_specs=(P(("pool", "frame", "tensor"), None), P(("pool", "frame", "tensor"), None)),
        check_vma=False,
    )
```

```python
import functools
import math

import jax
import jax.numpy as jnp
from jax import lax
from jax.experimental import pallas as pl
from jax.experimental.pallas import tpu as pltpu
from jax.sharding import PartitionSpec as P

STEPS = 50


def shifted(block, axis, distance):
    devices = range(lax.axis_size(axis))
    route = [(i - distance, i) for i in devices if i - distance in devices]
    return lax.ppermute(block, axis, route)


def time_embedding(t_index, w_mod):
    fraction = 1.0 - t_index[0].astype(jnp.float32) / STEPS
    following = fraction - 1.0 / STEPS
    sigma_now = 3.0 * fraction / (1.0 + 2.0 * fraction)
    sigma_next = 3.0 * following / (1.0 + 2.0 * following)
    half_width = w_mod.shape[0] // 2
    frequency = jnp.exp(
        -math.log(10000.0) * jnp.arange(half_width).astype(jnp.float32) / half_width
    )
    angles = 1000.0 * sigma_now * frequency
    embedding = jnp.concatenate([jnp.cos(angles), jnp.sin(angles)])
    return (jax.nn.silu(embedding).astype(jnp.bfloat16), sigma_next - sigma_now)


def modulation_of(t_index, w_mod):
    time_features, step_size = time_embedding(t_index, w_mod)
    shifts = jnp.dot(time_features[None, :], w_mod, preferred_element_type=jnp.float32)[0]
    return (shifts, step_size)


def own_state(key_heads, value_heads, cumulative):
    block_total = cumulative[:, -1]
    scaled = key_heads.astype(jnp.float32) * jnp.exp(block_total[:, None] - cumulative)[:, :, None]
    state_sum = jnp.einsum(
        "htd,hte->hde", scaled, value_heads.astype(jnp.float32), precision=lax.Precision.HIGHEST
    )
    return (block_total, state_sum)


def mix_block(query_heads, key_heads, value_heads, cumulative, labels, carried_state):
    factor = query_heads.shape[2] ** (-0.5)
    visible = labels[None, :] <= labels[:, None]
    decay = jnp.exp(jnp.minimum(cumulative[:, :, None] - cumulative[:, None, :], 0.0))
    weights = jnp.where(visible[None], decay, 0.0) * factor
    scores = jnp.einsum("hid,hjd->hij", query_heads, key_heads, preferred_element_type=jnp.float32)
    probs = (scores * weights).astype(jnp.bfloat16)
    inner_part = jnp.einsum("hij,hjd->hid", probs, value_heads, preferred_element_type=jnp.float32)
    carried = jnp.einsum(
        "hid,hde->hie",
        query_heads.astype(jnp.float32),
        carried_state,
        precision=lax.Precision.HIGHEST,
    )
    numerator = inner_part + carried * (jnp.exp(cumulative) * factor)[:, :, None]
    normed = numerator * lax.rsqrt(jnp.mean(numerator * numerator, axis=2, keepdims=True) + 1e-06)
    return normed.astype(jnp.bfloat16)


def layer_norm(hidden):
    centered = hidden - jnp.mean(hidden, axis=1, keepdims=True)
    variance = jnp.mean(centered * centered, axis=1, keepdims=True)
    return centered * lax.rsqrt(variance + 1e-06)


def by_collectives(
    latents, queries, keys, values, log_decay, block_ids, t_index, w_mod, w_out, w_up, w_down
):
    shifts, step_size = modulation_of(t_index, w_mod)
    width = latents.shape[1]
    head_count = log_decay.shape[0]
    token_count = log_decay.shape[1]
    head_size = queries.shape[1] // head_count

    def to_heads(rows_in):
        return rows_in.reshape(token_count, head_count, head_size).transpose(1, 0, 2)

    query_heads = to_heads(queries)
    key_heads = to_heads(keys)
    value_heads = to_heads(values)
    cumulative = jnp.cumsum(log_decay, axis=1)
    block_total, state_sum = own_state(key_heads, value_heads, cumulative)
    keep_factor = jnp.exp(block_total)[:, None, None]

    def relay(turn, incoming):
        return shifted(
            (keep_factor * incoming + state_sum).astype(jnp.bfloat16), "frame", 1
        ).astype(jnp.float32)

    carried_state = lax.fori_loop(0, lax.axis_size("frame") - 1, relay, jnp.zeros_like(state_sum))
    mixed = mix_block(query_heads, key_heads, value_heads, cumulative, block_ids, carried_state)
    mixed_rows = mixed.transpose(1, 0, 2).reshape(token_count, head_count * head_size)
    head_terms = jnp.dot(
        mixed_rows,
        lax.all_gather(w_out, "frame", axis=1, tiled=True),
        preferred_element_type=jnp.float32,
    )
    attention = lax.psum_scatter(
        head_terms.astype(jnp.bfloat16), "tensor", scatter_dimension=0, tiled=True
    ).astype(jnp.float32)
    hidden = latents.astype(jnp.float32) + shifts[3 * width :] * attention
    normed = (layer_norm(hidden) * (1.0 + shifts[width : 2 * width]) + shifts[:width]).astype(
        jnp.bfloat16
    )
    normed_all = lax.all_gather(normed, "tensor", axis=0, tiled=True)
    up_sums = jnp.dot(
        normed_all,
        lax.all_gather(w_up, "frame", axis=0, tiled=True),
        preferred_element_type=jnp.float32,
    )
    units = jax.nn.gelu(up_sums, approximate=True).astype(jnp.bfloat16)
    unit_terms = jnp.dot(
        units,
        lax.all_gather(w_down, "frame", axis=1, tiled=True),
        preferred_element_type=jnp.float32,
    )
    feed = lax.psum_scatter(
        unit_terms.astype(jnp.bfloat16), "tensor", scatter_dimension=0, tiled=True
    ).astype(jnp.float32)
    velocity = (hidden + shifts[2 * width : 3 * width] * feed).astype(jnp.bfloat16)
    advanced = (latents.astype(jnp.float32) + step_size * velocity.astype(jnp.float32)).astype(
        jnp.bfloat16
    )
    return (velocity, advanced)


MESH = pl.DeviceIdType.MESH


def at_most(count, value):
    return jnp.minimum(jnp.maximum(value, 0), count - 1)


def fused(
    sizes,
    q_ref, k_ref, v_ref, decay_ref, label_ref, lat_ref, feature_ref, step_ref,
    w_out_ref, w_up_ref, w_down_ref, w_mod_ref,
    velocity_ref, advanced_ref,
    out_buf, up_buf, down_buf, mod_buf, state_out, state_in, mixed,
    first, first_in, spread, second, second_in, hidden, attended, units_own, columns, shift_rows,
    own_sem, y_send, y_recv, x_send, x_recv, core_send, core_recv, state_sems,
    first_send, first_recv, spread_send, spread_recv, second_send, second_recv,
):
    ranks, slabs, head_count, head_size, rows, tokens, quarters = sizes
    z = lax.axis_index("tensor")
    f = lax.axis_index("frame")
    pool = lax.axis_index("pool")
    core = lax.rem(pool, 2)
    other_core = pool + 1 - 2 * core
    other_chip = lax.rem(pool + 2, 4)
    other_f = 1 - f
    factor = head_size ** (-0.5)

    barrier = pltpu.get_barrier_semaphore()
    pl.semaphore_signal(barrier, inc=1, device_id={"frame": other_f}, device_id_type=MESH)
    pl.semaphore_signal(barrier, inc=1, device_id={"pool": other_core}, device_id_type=MESH)
    pl.semaphore_signal(barrier, inc=1, device_id={"pool": other_chip}, device_id_type=MESH)

    @pl.when(z > 0)
    def _():
        pl.semaphore_signal(barrier, inc=1, device_id={"tensor": z - 1}, device_id_type=MESH)

    @pl.when(z < ranks - 1)
    def _():
        pl.semaphore_signal(barrier, inc=1, device_id={"tensor": z + 1}, device_id_type=MESH)

    sources = (w_out_ref, w_up_ref, w_down_ref)
    buffers = (out_buf, up_buf, down_buf)
    own_copies = [
        pltpu.make_async_copy(sources[i], buffers[i].at[f], own_sem.at[i]) for i in range(3)
    ]
    for copy in own_copies:
        copy.start()
    mod_copy = pltpu.make_async_copy(w_mod_ref, mod_buf, own_sem.at[3])
    mod_copy.start()

    earlier = (
        lax.broadcasted_iota(jnp.int32, (tokens, tokens), 0)
        <= lax.broadcasted_iota(jnp.int32, (tokens, tokens), 1)
    ).astype(jnp.float32).astype(jnp.bfloat16)
    rest = decay_ref[...]
    cum = jnp.zeros_like(rest)
    for _ in range(3):
        leading = rest.astype(jnp.bfloat16)
        rest = rest - leading.astype(jnp.float32)
        cum += jnp.dot(leading, earlier, preferred_element_type=jnp.float32)
    columns[...] = jnp.zeros_like(columns)
    columns[0:head_count, :] = cum
    columns[head_count : head_count + 1, :] = label_ref[...].astype(jnp.float32)
    cum_col = columns[...].T

    for h in range(head_count):
        part = slice(h * head_size, (h + 1) * head_size)
        row = cum[h : h + 1, :]
        total = row[:, tokens - 1 : tokens]
        scaled = (k_ref[part, :].astype(jnp.float32) * jnp.exp(total - row)).astype(jnp.bfloat16)
        state_out[h] = lax.dot_general(
            v_ref[part, :], scaled, (((1,), (1,)), ((), ())), preferred_element_type=jnp.float32
        ).astype(jnp.bfloat16)

    links = 3 + (z > 0).astype(jnp.int32) + (z < ranks - 1).astype(jnp.int32)
    pl.semaphore_wait(barrier, links)

    state_copy = pltpu.make_async_remote_copy(
        src_ref=state_out, dst_ref=state_in, send_sem=state_sems.at[0], recv_sem=state_sems.at[1],
        device_id={"frame": other_f}, device_id_type=MESH,
    )

    @pl.when(f == 0)
    def _():
        state_copy.start()
        state_in[...] = jnp.zeros_like(state_in)

    def across(i, quarter):
        part = pl.ds(*quarters[i][quarter])
        return pltpu.make_async_remote_copy(
            src_ref=sources[i].at[part], dst_ref=buffers[i].at[f, part],
            send_sem=y_send.at[i], recv_sem=y_recv.at[i],
            device_id={"frame": other_f}, device_id_type=MESH,
        )

    def arrived(i, quarter):
        part = pl.ds(*quarters[i][quarter])
        return pltpu.make_async_remote_copy(
            src_ref=sources[i].at[part], dst_ref=buffers[i].at[other_f, part],
            send_sem=y_send.at[i], recv_sem=y_recv.at[i],
            device_id={"frame": other_f}, device_id_type=MESH,
        )

    def region(i, quarter):
        return buffers[i].at[other_f, pl.ds(*quarters[i][quarter])]

    def to_chip(i, quarter):
        return pltpu.make_async_remote_copy(
            src_ref=region(i, quarter), dst_ref=region(i, quarter),
            send_sem=x_send.at[i], recv_sem=x_recv.at[i],
            device_id={"pool": other_chip}, device_id_type=MESH,
        )

    def to_core(i, quarter, turn):
        return pltpu.make_async_remote_copy(
            src_ref=region(i, quarter), dst_ref=region(i, quarter),
            send_sem=core_send.at[i, turn], recv_sem=core_recv.at[i, turn],
            device_id={"pool": other_core}, device_id_type=MESH,
        )

    def each_quarter(act):
        for quarter in range(4):
            @pl.when(pool == quarter)
            def _():
                act(quarter)

    each_quarter(lambda quarter: across(0, quarter).start())

    def pass_on(i):
        def act(quarter):
            arrived(i, quarter).wait_recv()
            to_chip(i, quarter).start()
            to_core(i, quarter, 0).start()
        each_quarter(act)

    def pass_round(i):
        def act(quarter):
            opposite = (quarter + 2) % 4
            to_chip(i, opposite).wait_recv()
            to_core(i, opposite, 1).start()
        each_quarter(act)

    def settle(i):
        def act(quarter):
            to_core(i, quarter ^ 1, 0).wait_recv()
            to_core(i, (quarter ^ 1) ^ 2, 1).wait_recv()
        own_copies[i].wait()
        each_quarter(act)

    visible = cum_col[:, head_count : head_count + 1] <= columns[head_count : head_count + 1, :]
    for h in range(head_count):
        part = slice(h * head_size, (h + 1) * head_size)
        qh = q_ref[part, :]
        scores = lax.dot_general(
            k_ref[part, :], qh, (((0,), (0,)), ((), ())), preferred_element_type=jnp.float32
        )
        row = cum[h : h + 1, :]
        decay = jnp.exp(jnp.minimum(row - cum_col[:, h : h + 1], 0.0))
        probs = (scores * (jnp.where(visible, decay, 0.0) * factor)).astype(jnp.bfloat16)
        inner = jnp.dot(v_ref[part, :], probs, preferred_element_type=jnp.float32)
        if h == 0:
            @pl.when(f > 0)
            def _():
                state_copy.wait_recv()
        carried = jnp.dot(state_in[h], qh, preferred_element_type=jnp.float32)
        numerator = inner + carried * (jnp.exp(row) * factor)
        power = jnp.mean(numerator * numerator, axis=0, keepdims=True)
        mixed[:, part] = (numerator * lax.rsqrt(power + 1e-06)).T.astype(jnp.bfloat16)

    pass_on(0)
    each_quarter(lambda quarter: across(1, quarter).start())
    pass_round(0)
    settle(0)
    each_quarter(lambda quarter: across(2, quarter).start())

    def rows_of(d):
        return pl.ds(pl.multiple_of(d * rows, rows), rows)

    half = rows // 2

    def hop(buf, landing, send_sem, recv_sem, way, d, s, r):
        to = at_most(ranks, z + 1 - 2 * way)
        part = pl.ds(r * half, half)
        return pltpu.make_async_remote_copy(
            src_ref=buf.at[d, s, part], dst_ref=landing.at[way, d, s, part],
            send_sem=send_sem.at[d, s, r], recv_sem=recv_sem.at[way, d, s, r],
            device_id={"tensor": to}, device_id_type=MESH,
        )

    def hop1(way, d, s, r):
        return hop(first, first_in, first_send, first_recv, way, d, s, r)

    def hop2(way, d, s, r):
        return hop(second, second_in, second_send, second_recv, way, d, s, r)

    def send_slab(hop_of, buf, landing, way, d, s, before, follows):
        earlier_d = at_most(ranks, jnp.where(s > 0, d, before))
        earlier_s = jnp.where(s > 0, s - 1, slabs - 1)
        for r in range(2):
            part = pl.ds(r * half, half)

            @pl.when(has_upstream(way))
            def _():
                hop_of(way, d, s, r).wait_recv()
                buf[d, s, part] = (
                    buf[d, s, part].astype(jnp.float32) + landing[way, d, s, part].astype(jnp.float32)
                ).astype(jnp.bfloat16)

            @pl.when((s > 0) | follows)
            def _():
                hop_of(way, earlier_d, earlier_s, r).wait_send()

            hop_of(way, d, s, r).start()

    def last_left(hop_of, way, d):
        @pl.when(has_downstream(way))
        def _():
            for r in range(2):
                hop_of(way, at_most(ranks, d), slabs - 1, r).wait_send()

    def has_downstream(way):
        return jnp.where(way == 0, z < ranks - 1, z > 0)

    def has_upstream(way):
        return jnp.where(way == 0, z > 0, z < ranks - 1)

    def first_turn(turn, carry):
        step = turn // 2
        near = jnp.where(z < ranks // 2, 0, 1)
        way = lax.rem(turn + near, 2)
        d = jnp.where(way == 0, ranks - 1 - step, step)
        active = jnp.where(way == 0, d > z, d < z)

        @pl.when(active)
        def _():
            def slab(s, c):
                part = jnp.dot(mixed[rows_of(d), :], out_buf[s], preferred_element_type=jnp.float32)
                first[d, s] = part.astype(jnp.bfloat16)

                send_slab(hop1, first, first_in, way, d, s, jnp.where(way == 0, d + 1, d - 1), step > 0)
                return c

            lax.fori_loop(0, slabs, slab, 0)

        return carry

    lax.fori_loop(0, 2 * (ranks - 1), first_turn, 0)

    def own_slab(s, c):
        part = jnp.dot(mixed[rows_of(z), :], out_buf[s], preferred_element_type=jnp.float32)
        attended[s] = part.astype(jnp.bfloat16).astype(jnp.float32)
        return c

    lax.fori_loop(0, slabs, own_slab, 0)
    pass_on(1)

    mod_copy.wait()
    shift_rows[...] = jnp.dot(feature_ref[...], mod_buf[...], preferred_element_type=jnp.float32)
    piece = hidden.shape[2]

    def shift(kind, s):
        start = (kind * slabs + s) * piece
        return shift_rows[0:1, start : start + piece]

    def lat(s):
        return lat_ref[s * piece : (s + 1) * piece, :].astype(jnp.float32).T

    pass_round(1)

    def gather_sums(hop_of, landing, target):
        for way in range(2):
            @pl.when(has_upstream(way))
            def _():
                for s in range(slabs):
                    for r in range(2):
                        hop_of(way, z, s, r).wait_recv()
                    target[s] += landing[way, z, s].astype(jnp.float32)

    gather_sums(hop1, first_in, attended)

    total = jnp.zeros((rows, 1), jnp.float32)
    for s in range(slabs):
        value = lat(s) + shift(3, s) * attended[s]
        hidden[s] = value
        total += jnp.sum(value, axis=1, keepdims=True)
    width = slabs * hidden.shape[2]
    mean = total / width
    squares = jnp.zeros((rows, 1), jnp.float32)
    for s in range(slabs):
        centered = hidden[s] - mean
        squares += jnp.sum(centered * centered, axis=1, keepdims=True)
    inverse = lax.rsqrt(squares / width + 1e-06)
    for s in range(slabs):
        spread[z, s] = (
            (hidden[s] - mean) * inverse * (1.0 + shift(1, s)) + shift(0, s)
        ).astype(jnp.bfloat16)

    def relay(way, c, s):
        to = at_most(ranks, z + 1 - 2 * way)
        return pltpu.make_async_remote_copy(
            src_ref=spread.at[c, s], dst_ref=spread.at[c, s],
            send_sem=spread_send.at[way, c, s], recv_sem=spread_recv.at[c, s],
            device_id={"tensor": to}, device_id_type=MESH,
        )

    for way in range(2):
        last_left(hop1, way, z + 1 - 2 * way)

    for way in range(2):
        @pl.when(has_downstream(way))
        def _():
            for s in range(slabs):
                relay(way, z, s).start()

    settle(1)

    def up_side(c):
        acc = jnp.dot(spread[c, 0], up_buf[0], preferred_element_type=jnp.float32)
        for s in range(1, slabs):
            acc += jnp.dot(spread[c, s], up_buf[s], preferred_element_type=jnp.float32)
        return jax.nn.gelu(acc, approximate=True).astype(jnp.bfloat16)

    units_own[...] = up_side(z)
    pass_on(2)
    pass_round(2)

    def tick(k, carry):
        def chunk_of(way):
            return jnp.where(way == 0, z - k, z + k)

        def arrival(way, c0):
            c = chunk_of(way)

            @pl.when((c >= 0) & (c < ranks))
            def _():
                for s in range(slabs):
                    relay(way, c, s).wait_recv()

                    @pl.when(has_downstream(way))
                    def _():
                        relay(way, c, s).start()

            return c0

        def work(way, c0):
            c = chunk_of(way)

            @pl.when((c >= 0) & (c < ranks))
            def _():
                units = up_side(c)

                @pl.when((k == 1) & ((way == 0) | (z == 0)))
                def _():
                    settle(2)

                for s in range(slabs):
                    second[c, s] = jnp.dot(
                        units, down_buf[s], preferred_element_type=jnp.float32
                    ).astype(jnp.bfloat16)

            return c0

        @pl.when(k < ranks)
        def _():
            lax.fori_loop(0, 2, arrival, 0)
            lax.fori_loop(0, 2, work, 0)

        def sending(way, c0):
            place = jnp.where(way == 0, z, ranks - 1 - z)
            ahead = k - place
            d = jnp.where(way == 0, ahead, ranks - 1 - ahead)

            @pl.when((ahead > place) & (ahead < ranks))
            def _():
                def slab(s, c1):
                    send_slab(
                        hop2, second, second_in, way, d, s,
                        jnp.where(way == 0, d - 1, d + 1), ahead > place + 1,
                    )
                    return c1

                lax.fori_loop(0, slabs, slab, 0)

            return c0

        lax.fori_loop(0, 2, sending, 0)
        return carry

    lax.fori_loop(1, 2 * ranks - 2, tick, 0)

    for s in range(slabs):
        attended[s] = (
            jnp.dot(units_own[...], down_buf[s], preferred_element_type=jnp.float32)
            .astype(jnp.bfloat16)
            .astype(jnp.float32)
        )
    gather_sums(hop2, second_in, attended)
    step = step_ref[...]
    for s in range(slabs):
        velocity = (hidden[s] + shift(2, s) * attended[s]).astype(jnp.bfloat16).astype(jnp.float32)
        part = slice(s * piece, (s + 1) * piece)
        velocity = velocity.T
        velocity_ref[part, :] = velocity.astype(jnp.bfloat16)
        advanced_ref[part, :] = (
            lat_ref[part, :].astype(jnp.float32) + step * velocity
        ).astype(jnp.bfloat16)

    @pl.when(f == 0)
    def _():
        state_copy.wait_send()

    for i in range(3):
        def left(quarter):
            across(i, quarter).wait_send()
            to_chip(i, quarter).wait_send()
            to_core(i, quarter, 0).wait_send()
            to_core(i, (quarter + 2) % 4, 1).wait_send()
        each_quarter(left)

    last_left(hop2, 0, ranks - 1)
    last_left(hop2, 1, 0)

    def drain(d, carry):
        def slab(s, c):
            def direction(way, c1):
                came = jnp.where(way == 0, d <= z, d >= z)

                @pl.when(came & has_downstream(way))
                def _():
                    relay(way, d, s).wait_send()

                return c1

            lax.fori_loop(0, 2, direction, 0)
            return c

        lax.fori_loop(0, slabs, slab, 0)
        return carry

    lax.fori_loop(0, ranks, drain, 0)


def fits(latents, queries, log_decay, w_out, w_up, w_down):
    frames, ranks, pools = (lax.axis_size(a) for a in ("frame", "tensor", "pool"))
    rows, tokens = latents.shape[0], queries.shape[0]
    return (
        frames == 2
        and pools == 4
        and ranks > 1
        and rows % 128 == 0
        and latents.shape[1] % (16 * frames) == 0
        and log_decay.shape[0] < 8
        and rows * ranks == tokens
        and rows % 16 == 0
        and all(w.shape[0] % 16 == 0 and w.shape[0] >= 64 for w in (w_out, w_up, w_down))
        and w_up.shape[0] == w_out.shape[1] == w_down.shape[1]
        and queries.shape[1] // log_decay.shape[0] % 16 == 0
    )


def on_device(
    latents, queries, keys, values, log_decay, block_ids, t_index, w_mod, w_out, w_up, w_down
):
    if not fits(latents, queries, log_decay, w_out, w_up, w_down):
        return by_collectives(
            latents, queries, keys, values, log_decay, block_ids, t_index, w_mod, w_out, w_up, w_down
        )
    ranks, slabs = lax.axis_size("tensor"), lax.axis_size("frame")
    rows, width = latents.shape
    piece = width // slabs
    tokens, features = queries.shape
    head_count = log_decay.shape[0]
    head_size = features // head_count
    time_features, step_size = time_embedding(t_index, w_mod)

    def split(count):
        edges = [count // 16 * i // 4 * 16 for i in range(5)]
        return tuple((edges[i], edges[i + 1] - edges[i]) for i in range(4))

    quarters = tuple(split(w.shape[0]) for w in (w_out, w_up, w_down))
    sizes = (ranks, slabs, head_count, head_size, rows, tokens, quarters)
    block = (ranks, slabs, rows, piece)
    vmem = pl.BlockSpec(memory_space=pltpu.VMEM)
    anywhere = pl.BlockSpec(memory_space=pl.ANY)
    dma = pltpu.SemaphoreType.DMA
    velocity, advanced = pl.pallas_call(
        functools.partial(fused, sizes),
        out_shape=[jax.ShapeDtypeStruct((width, rows), jnp.bfloat16)] * 2,
        in_specs=[vmem] * 8 + [anywhere] * 4,
        out_specs=[vmem] * 2,
        scratch_shapes=[
            pltpu.VMEM((slabs,) + w_out.shape, jnp.bfloat16),
            pltpu.VMEM((slabs,) + w_up.shape, jnp.bfloat16),
            pltpu.VMEM((slabs,) + w_down.shape, jnp.bfloat16),
            pltpu.VMEM(w_mod.shape, jnp.bfloat16),
            pltpu.VMEM((head_count, head_size, head_size), jnp.bfloat16),
            pltpu.VMEM((head_count, head_size, head_size), jnp.bfloat16),
            pltpu.VMEM((tokens, features), jnp.bfloat16),
            pltpu.VMEM(block, jnp.bfloat16),
            pltpu.VMEM((2,) + block, jnp.bfloat16),
            pltpu.VMEM(block, jnp.bfloat16),
            pltpu.VMEM(block, jnp.bfloat16),
            pltpu.VMEM((2,) + block, jnp.bfloat16),
            pltpu.VMEM((slabs, rows, piece), jnp.float32),
            pltpu.VMEM((slabs, rows, piece), jnp.float32),
            pltpu.VMEM((rows, w_up.shape[1]), jnp.bfloat16),
            pltpu.VMEM((8, tokens), jnp.float32),
            pltpu.VMEM((8, w_mod.shape[1]), jnp.float32),
            dma((4,)), dma((3,)), dma((3,)), dma((3,)), dma((3,)), dma((3, 2)), dma((3, 2)), dma((2,)),
            dma((ranks, slabs, 2)), dma((2, ranks, slabs, 2)),
            dma((2, ranks, slabs)), dma((ranks, slabs)),
            dma((ranks, slabs, 2)), dma((2, ranks, slabs, 2)),
        ],
        compiler_params=pltpu.CompilerParams(
            collective_id=0, has_side_effects=True, vmem_limit_bytes=56 * 1024 * 1024
        ),
        name="sublayers",
    )(
        queries.T, keys.T, values.T, log_decay, block_ids[None, :], latents.T,
        jnp.broadcast_to(time_features, (8, time_features.shape[0])), step_size.reshape(1, 1),
        w_out, w_up, w_down, w_mod,
    )
    return (velocity.T, advanced.T)


def solution(mesh):
    return jax.shard_map(
        on_device,
        mesh=mesh,
        in_specs=(
            P(("pool", "frame", "tensor"), None),
            P(("pool", "frame"), "tensor"),
            P(("pool", "frame"), "tensor"),
            P(("pool", "frame"), "tensor"),
            P("tensor", ("pool", "frame")),
            P(("pool", "frame")),
            P("pool"),
            P(),
            P("tensor", "frame"),
            P("frame", "tensor"),
            P("tensor", "frame"),
        ),
        out_specs=(P(("pool", "frame", "tensor"), None), P(("pool", "frame", "tensor"), None)),
        check_vma=False,
    )
```

```python
import functools
import math

import jax
import jax.numpy as jnp
from jax import lax
from jax.experimental import pallas as pl
from jax.experimental.pallas import tpu as pltpu
from jax.sharding import PartitionSpec as P

STEPS = 50


def shifted(block, axis, distance):
    devices = range(lax.axis_size(axis))
    route = [(i - distance, i) for i in devices if i - distance in devices]
    return lax.ppermute(block, axis, route)


def time_embedding(t_index, w_mod):
    fraction = 1.0 - t_index[0].astype(jnp.float32) / STEPS
    following = fraction - 1.0 / STEPS
    sigma_now = 3.0 * fraction / (1.0 + 2.0 * fraction)
    sigma_next = 3.0 * following / (1.0 + 2.0 * following)
    half_width = w_mod.shape[0] // 2
    frequency = jnp.exp(
        -math.log(10000.0) * jnp.arange(half_width).astype(jnp.float32) / half_width
    )
    angles = 1000.0 * sigma_now * frequency
    embedding = jnp.concatenate([jnp.cos(angles), jnp.sin(angles)])
    return (jax.nn.silu(embedding).astype(jnp.bfloat16), sigma_next - sigma_now)


def modulation_of(t_index, w_mod):
    time_features, step_size = time_embedding(t_index, w_mod)
    shifts = jnp.dot(time_features[None, :], w_mod, preferred_element_type=jnp.float32)[0]
    return (shifts, step_size)


def own_state(key_heads, value_heads, cumulative):
    block_total = cumulative[:, -1]
    scaled = key_heads.astype(jnp.float32) * jnp.exp(block_total[:, None] - cumulative)[:, :, None]
    state_sum = jnp.einsum(
        "htd,hte->hde", scaled, value_heads.astype(jnp.float32), precision=lax.Precision.HIGHEST
    )
    return (block_total, state_sum)


def mix_block(query_heads, key_heads, value_heads, cumulative, labels, carried_state):
    factor = query_heads.shape[2] ** (-0.5)
    visible = labels[None, :] <= labels[:, None]
    decay = jnp.exp(jnp.minimum(cumulative[:, :, None] - cumulative[:, None, :], 0.0))
    weights = jnp.where(visible[None], decay, 0.0) * factor
    scores = jnp.einsum("hid,hjd->hij", query_heads, key_heads, preferred_element_type=jnp.float32)
    probs = (scores * weights).astype(jnp.bfloat16)
    inner_part = jnp.einsum("hij,hjd->hid", probs, value_heads, preferred_element_type=jnp.float32)
    carried = jnp.einsum(
        "hid,hde->hie",
        query_heads.astype(jnp.float32),
        carried_state,
        precision=lax.Precision.HIGHEST,
    )
    numerator = inner_part + carried * (jnp.exp(cumulative) * factor)[:, :, None]
    normed = numerator * lax.rsqrt(jnp.mean(numerator * numerator, axis=2, keepdims=True) + 1e-06)
    return normed.astype(jnp.bfloat16)


def layer_norm(hidden):
    centered = hidden - jnp.mean(hidden, axis=1, keepdims=True)
    variance = jnp.mean(centered * centered, axis=1, keepdims=True)
    return centered * lax.rsqrt(variance + 1e-06)


def by_collectives(
    latents, queries, keys, values, log_decay, block_ids, t_index, w_mod, w_out, w_up, w_down
):
    shifts, step_size = modulation_of(t_index, w_mod)
    width = latents.shape[1]
    head_count = log_decay.shape[0]
    token_count = log_decay.shape[1]
    head_size = queries.shape[1] // head_count

    def to_heads(rows_in):
        return rows_in.reshape(token_count, head_count, head_size).transpose(1, 0, 2)

    query_heads = to_heads(queries)
    key_heads = to_heads(keys)
    value_heads = to_heads(values)
    cumulative = jnp.cumsum(log_decay, axis=1)
    block_total, state_sum = own_state(key_heads, value_heads, cumulative)
    keep_factor = jnp.exp(block_total)[:, None, None]

    def relay(turn, incoming):
        return shifted(
            (keep_factor * incoming + state_sum).astype(jnp.bfloat16), "frame", 1
        ).astype(jnp.float32)

    carried_state = lax.fori_loop(0, lax.axis_size("frame") - 1, relay, jnp.zeros_like(state_sum))
    mixed = mix_block(query_heads, key_heads, value_heads, cumulative, block_ids, carried_state)
    mixed_rows = mixed.transpose(1, 0, 2).reshape(token_count, head_count * head_size)
    head_terms = jnp.dot(
        mixed_rows,
        lax.all_gather(w_out, "frame", axis=1, tiled=True),
        preferred_element_type=jnp.float32,
    )
    attention = lax.psum_scatter(
        head_terms.astype(jnp.bfloat16), "tensor", scatter_dimension=0, tiled=True
    ).astype(jnp.float32)
    hidden = latents.astype(jnp.float32) + shifts[3 * width :] * attention
    normed = (layer_norm(hidden) * (1.0 + shifts[width : 2 * width]) + shifts[:width]).astype(
        jnp.bfloat16
    )
    normed_all = lax.all_gather(normed, "tensor", axis=0, tiled=True)
    up_sums = jnp.dot(
        normed_all,
        lax.all_gather(w_up, "frame", axis=0, tiled=True),
        preferred_element_type=jnp.float32,
    )
    units = jax.nn.gelu(up_sums, approximate=True).astype(jnp.bfloat16)
    unit_terms = jnp.dot(
        units,
        lax.all_gather(w_down, "frame", axis=1, tiled=True),
        preferred_element_type=jnp.float32,
    )
    feed = lax.psum_scatter(
        unit_terms.astype(jnp.bfloat16), "tensor", scatter_dimension=0, tiled=True
    ).astype(jnp.float32)
    velocity = (hidden + shifts[2 * width : 3 * width] * feed).astype(jnp.bfloat16)
    advanced = (latents.astype(jnp.float32) + step_size * velocity.astype(jnp.float32)).astype(
        jnp.bfloat16
    )
    return (velocity, advanced)


MESH = pl.DeviceIdType.MESH


def at_most(count, value):
    return jnp.minimum(jnp.maximum(value, 0), count - 1)


def fused(
    sizes,
    q_ref, k_ref, v_ref, decay_ref, label_ref, lat_ref, feature_ref, step_ref,
    w_out_ref, w_up_ref, w_down_ref, w_mod_ref,
    velocity_ref, advanced_ref,
    out_buf, up_buf, down_buf, mod_buf, state_out, state_in, mixed,
    first, first_in, spread, second, second_in, hidden, attended, units_own, columns, down_columns, key_rows, shift_rows,
    own_sem, y_send, y_recv, x_send, x_recv, core_send, core_recv, state_sems,
    first_send, first_recv, spread_send, spread_recv, second_send, second_recv,
):
    ranks, slabs, head_count, head_size, rows, tokens, quarters = sizes
    z = lax.axis_index("tensor")
    f = lax.axis_index("frame")
    pool = lax.axis_index("pool")
    core = lax.rem(pool, 2)
    other_core = pool + 1 - 2 * core
    other_chip = lax.rem(pool + 2, 4)
    other_f = 1 - f
    factor = head_size ** (-0.5)

    barrier = pltpu.get_barrier_semaphore()
    pl.semaphore_signal(barrier, inc=1, device_id={"frame": other_f}, device_id_type=MESH)
    pl.semaphore_signal(barrier, inc=1, device_id={"pool": other_core}, device_id_type=MESH)
    pl.semaphore_signal(barrier, inc=1, device_id={"pool": other_chip}, device_id_type=MESH)

    @pl.when(z > 0)
    def _():
        pl.semaphore_signal(barrier, inc=1, device_id={"tensor": z - 1}, device_id_type=MESH)

    @pl.when(z < ranks - 1)
    def _():
        pl.semaphore_signal(barrier, inc=1, device_id={"tensor": z + 1}, device_id_type=MESH)

    sources = (w_out_ref, w_up_ref, w_down_ref)
    buffers = (out_buf, up_buf, down_buf)
    own_copies = [
        pltpu.make_async_copy(sources[i], buffers[i].at[f], own_sem.at[i]) for i in range(3)
    ]
    for copy in own_copies:
        copy.start()
    mod_copy = pltpu.make_async_copy(w_mod_ref, mod_buf, own_sem.at[3])
    mod_copy.start()

    earlier = (
        lax.broadcasted_iota(jnp.int32, (tokens, tokens), 0)
        <= lax.broadcasted_iota(jnp.int32, (tokens, tokens), 1)
    ).astype(jnp.float32).astype(jnp.bfloat16)
    rest = decay_ref[...]
    cum = jnp.zeros_like(rest)
    for _ in range(3):
        leading = rest.astype(jnp.bfloat16)
        rest = rest - leading.astype(jnp.float32)
        cum += jnp.dot(leading, earlier, preferred_element_type=jnp.float32)
    columns[...] = jnp.zeros_like(columns)
    columns[0:head_count, :] = cum
    columns[head_count : head_count + 1, :] = label_ref[...].astype(jnp.float32)
    down_columns[...] = columns[...].T

    for h in range(head_count):
        part = slice(h * head_size, (h + 1) * head_size)
        row = cum[h : h + 1, :]
        total = row[:, tokens - 1 : tokens]
        keys = k_ref[part, :].astype(jnp.float32)
        key_rows[h] = keys.T.astype(jnp.bfloat16)
        scaled = (keys * jnp.exp(total - row)).astype(jnp.bfloat16)
        state_out[h] = lax.dot_general(
            v_ref[part, :], scaled, (((1,), (1,)), ((), ())), preferred_element_type=jnp.float32
        ).astype(jnp.bfloat16)

    links = 3 + (z > 0).astype(jnp.int32) + (z < ranks - 1).astype(jnp.int32)
    pl.semaphore_wait(barrier, links)

    state_copy = pltpu.make_async_remote_copy(
        src_ref=state_out, dst_ref=state_in, send_sem=state_sems.at[0], recv_sem=state_sems.at[1],
        device_id={"frame": other_f}, device_id_type=MESH,
    )

    @pl.when(f == 0)
    def _():
        state_copy.start()
        state_in[...] = jnp.zeros_like(state_in)

    def across(i, quarter):
        part = pl.ds(*quarters[i][quarter])
        return pltpu.make_async_remote_copy(
            src_ref=sources[i].at[part], dst_ref=buffers[i].at[f, part],
            send_sem=y_send.at[i], recv_sem=y_recv.at[i],
            device_id={"frame": other_f}, device_id_type=MESH,
        )

    def arrived(i, quarter):
        part = pl.ds(*quarters[i][quarter])
        return pltpu.make_async_remote_copy(
            src_ref=sources[i].at[part], dst_ref=buffers[i].at[other_f, part],
            send_sem=y_send.at[i], recv_sem=y_recv.at[i],
            device_id={"frame": other_f}, device_id_type=MESH,
        )

    def region(i, quarter):
        return buffers[i].at[other_f, pl.ds(*quarters[i][quarter])]

    def to_chip(i, quarter):
        return pltpu.make_async_remote_copy(
            src_ref=region(i, quarter), dst_ref=region(i, quarter),
            send_sem=x_send.at[i], recv_sem=x_recv.at[i],
            device_id={"pool": other_chip}, device_id_type=MESH,
        )

    def to_core(i, quarter, turn):
        return pltpu.make_async_remote_copy(
            src_ref=region(i, quarter), dst_ref=region(i, quarter),
            send_sem=core_send.at[i, turn], recv_sem=core_recv.at[i, turn],
            device_id={"pool": other_core}, device_id_type=MESH,
        )

    def each_quarter(act):
        for quarter in range(4):
            @pl.when(pool == quarter)
            def _():
                act(quarter)

    each_quarter(lambda quarter: across(0, quarter).start())

    def pass_on(i):
        def act(quarter):
            arrived(i, quarter).wait_recv()
            to_chip(i, quarter).start()
            to_core(i, quarter, 0).start()
        each_quarter(act)

    def pass_round(i):
        def act(quarter):
            opposite = (quarter + 2) % 4
            to_chip(i, opposite).wait_recv()
            to_core(i, opposite, 1).start()
        each_quarter(act)

    def settle(i):
        def act(quarter):
            to_core(i, quarter ^ 1, 0).wait_recv()
            to_core(i, (quarter ^ 1) ^ 2, 1).wait_recv()
        each_quarter(act)

    @pl.when(f > 0)
    def _():
        state_copy.wait_recv()

    def attend(d):
        block = pl.ds(pl.multiple_of(d * rows, rows), rows)
        visible = (
            down_columns[:, head_count : head_count + 1] <= columns[head_count : head_count + 1, block]
        )
        for h in range(head_count):
            part = slice(h * head_size, (h + 1) * head_size)
            qh = q_ref[part, block]
            scores = jnp.dot(key_rows[h], qh, preferred_element_type=jnp.float32)
            row = columns[h : h + 1, block]
            decay = jnp.exp(jnp.minimum(row - down_columns[:, h : h + 1], 0.0))
            probs = (scores * (jnp.where(visible, decay, 0.0) * factor)).astype(jnp.bfloat16)
            inner = jnp.dot(v_ref[part, :], probs, preferred_element_type=jnp.float32)
            carried = jnp.dot(state_in[h], qh, preferred_element_type=jnp.float32)
            numerator = inner + carried * (jnp.exp(row) * factor)
            power = jnp.mean(numerator * numerator, axis=0, keepdims=True)
            mixed[block, part] = (numerator * lax.rsqrt(power + 1e-06)).T.astype(jnp.bfloat16)

    own_copies[0].wait()

    def rows_of(d):
        return pl.ds(pl.multiple_of(d * rows, rows), rows)

    def hop(buf, landing, send_sem, recv_sem, way, d, s):
        to = at_most(ranks, z + 1 - 2 * way)
        return pltpu.make_async_remote_copy(
            src_ref=buf.at[d, s], dst_ref=landing.at[way, d, s],
            send_sem=send_sem.at[d, s], recv_sem=recv_sem.at[way, d, s],
            device_id={"tensor": to}, device_id_type=MESH,
        )

    def hop1(way, d, s):
        return hop(first, first_in, first_send, first_recv, way, d, s)

    def hop2(way, d, s):
        return hop(second, second_in, second_send, second_recv, way, d, s)

    def has_upstream(way):
        return jnp.where(way == 0, z > 0, z < ranks - 1)

    def first_turn(turn, s, fresh):
        step = turn // 2
        near = jnp.where(z < ranks // 2, 0, 1)
        way = lax.rem(turn + near, 2)
        d = jnp.where(way == 0, ranks - 1 - step, step)
        active = jnp.where(way == 0, d > z, d < z)

        @pl.when(active)
        def _():
            if fresh:
                attend(d)
            part = jnp.dot(mixed[rows_of(d), :], out_buf[s], preferred_element_type=jnp.float32)
            first[d, s] = part.astype(jnp.bfloat16)

            @pl.when(has_upstream(way))
            def _():
                hop1(way, d, s).wait_recv()
                first[d, s] = (
                    first[d, s].astype(jnp.float32) + first_in[way, d, s].astype(jnp.float32)
                ).astype(jnp.bfloat16)

            hop1(way, d, s).start()

    def own_slab(s):
        part = jnp.dot(mixed[rows_of(z), :], out_buf[s], preferred_element_type=jnp.float32)
        attended[s] = part.astype(jnp.bfloat16).astype(jnp.float32)

    def near_columns(turn, carry):
        first_turn(turn, f, True)

        @pl.when(turn == ranks // 2 - 1)
        def _():
            pass_on(0)
            each_quarter(lambda quarter: across(1, quarter).start())

        @pl.when(turn == ranks - 1)
        def _():
            pass_round(0)
            each_quarter(lambda quarter: across(2, quarter).start())

        return carry

    lax.fori_loop(0, 2 * (ranks - 1), near_columns, 0)
    attend(z)
    own_slab(f)
    settle(0)

    def far_columns(turn, carry):
        first_turn(turn, other_f, False)
        return carry

    lax.fori_loop(0, 2 * (ranks - 1), far_columns, 0)
    own_slab(other_f)
    pass_on(1)

    mod_copy.wait()
    shift_rows[...] = jnp.dot(feature_ref[...], mod_buf[...], preferred_element_type=jnp.float32)
    piece = hidden.shape[2]

    def shift(kind, s):
        start = (kind * slabs + s) * piece
        return shift_rows[0:1, start : start + piece]

    def lat(s):
        return lat_ref[s * piece : (s + 1) * piece, :].astype(jnp.float32).T

    pass_round(1)

    def gather_sums(hop_of, landing, target):
        for way in range(2):
            @pl.when(has_upstream(way))
            def _():
                for s in range(slabs):
                    hop_of(way, z, s).wait_recv()
                    target[s] += landing[way, z, s].astype(jnp.float32)

    gather_sums(hop1, first_in, attended)

    total = jnp.zeros((rows, 1), jnp.float32)
    for s in range(slabs):
        value = lat(s) + shift(3, s) * attended[s]
        hidden[s] = value
        total += jnp.sum(value, axis=1, keepdims=True)
    width = slabs * hidden.shape[2]
    mean = total / width
    squares = jnp.zeros((rows, 1), jnp.float32)
    for s in range(slabs):
        centered = hidden[s] - mean
        squares += jnp.sum(centered * centered, axis=1, keepdims=True)
    inverse = lax.rsqrt(squares / width + 1e-06)
    for s in range(slabs):
        spread[z, s] = (
            (hidden[s] - mean) * inverse * (1.0 + shift(1, s)) + shift(0, s)
        ).astype(jnp.bfloat16)

    def relay(way, c, s):
        to = at_most(ranks, z + 1 - 2 * way)
        return pltpu.make_async_remote_copy(
            src_ref=spread.at[c, s], dst_ref=spread.at[c, s],
            send_sem=spread_send.at[way, c, s], recv_sem=spread_recv.at[c, s],
            device_id={"tensor": to}, device_id_type=MESH,
        )

    def has_downstream(way):
        return jnp.where(way == 0, z < ranks - 1, z > 0)

    for way in range(2):
        @pl.when(has_downstream(way))
        def _():
            for s in range(slabs):
                relay(way, z, s).start()

    own_copies[1].wait()
    settle(1)

    def up_side(c):
        acc = jnp.dot(spread[c, 0], up_buf[0], preferred_element_type=jnp.float32)
        for s in range(1, slabs):
            acc += jnp.dot(spread[c, s], up_buf[s], preferred_element_type=jnp.float32)
        return jax.nn.gelu(acc, approximate=True).astype(jnp.bfloat16)

    units_own[...] = up_side(z)
    pass_on(2)
    pass_round(2)

    def tick(k, carry):
        def chunk_of(way):
            return jnp.where(way == 0, z - k, z + k)

        def arrival(way, c0):
            c = chunk_of(way)

            @pl.when((c >= 0) & (c < ranks))
            def _():
                for s in range(slabs):
                    relay(way, c, s).wait_recv()

                    @pl.when(has_downstream(way))
                    def _():
                        relay(way, c, s).start()

            return c0

        def work(way, c0):
            c = chunk_of(way)

            @pl.when((c >= 0) & (c < ranks))
            def _():
                units = up_side(c)

                @pl.when((k == 1) & ((way == 0) | (z == 0)))
                def _():
                    own_copies[2].wait()
                    settle(2)

                for s in range(slabs):
                    second[c, s] = jnp.dot(
                        units, down_buf[s], preferred_element_type=jnp.float32
                    ).astype(jnp.bfloat16)

            return c0

        @pl.when(k < ranks)
        def _():
            lax.fori_loop(0, 2, arrival, 0)
            lax.fori_loop(0, 2, work, 0)

        def sending(way, c0):
            place = jnp.where(way == 0, z, ranks - 1 - z)
            ahead = k - place
            d = jnp.where(way == 0, ahead, ranks - 1 - ahead)

            @pl.when((ahead > place) & (ahead < ranks))
            def _():
                def slab(s, c1):
                    @pl.when(has_upstream(way))
                    def _():
                        hop2(way, d, s).wait_recv()
                        second[d, s] = (
                            second[d, s].astype(jnp.float32) + second_in[way, d, s].astype(jnp.float32)
                        ).astype(jnp.bfloat16)

                    hop2(way, d, s).start()
                    return c1

                lax.fori_loop(0, slabs, slab, 0)

            return c0

        lax.fori_loop(0, 2, sending, 0)
        return carry

    lax.fori_loop(1, 2 * ranks - 2, tick, 0)

    for s in range(slabs):
        attended[s] = (
            jnp.dot(units_own[...], down_buf[s], preferred_element_type=jnp.float32)
            .astype(jnp.bfloat16)
            .astype(jnp.float32)
        )
    gather_sums(hop2, second_in, attended)
    step = step_ref[...]
    for s in range(slabs):
        velocity = (hidden[s] + shift(2, s) * attended[s]).astype(jnp.bfloat16).astype(jnp.float32)
        part = slice(s * piece, (s + 1) * piece)
        velocity = velocity.T
        velocity_ref[part, :] = velocity.astype(jnp.bfloat16)
        advanced_ref[part, :] = (
            lat_ref[part, :].astype(jnp.float32) + step * velocity
        ).astype(jnp.bfloat16)

    @pl.when(f == 0)
    def _():
        state_copy.wait_send()

    for i in range(3):
        def left(quarter):
            across(i, quarter).wait_send()
            to_chip(i, quarter).wait_send()
            to_core(i, quarter, 0).wait_send()
            to_core(i, (quarter + 2) % 4, 1).wait_send()
        each_quarter(left)

    def drain(d, carry):
        def slab(s, c):
            @pl.when(d != z)
            def _():
                way = jnp.where(d > z, 0, 1)
                hop1(way, d, s).wait_send()
                hop2(way, d, s).wait_send()

            def direction(way, c1):
                came = jnp.where(way == 0, d <= z, d >= z)

                @pl.when(came & has_downstream(way))
                def _():
                    relay(way, d, s).wait_send()

                return c1

            lax.fori_loop(0, 2, direction, 0)
            return c

        lax.fori_loop(0, slabs, slab, 0)
        return carry

    lax.fori_loop(0, ranks, drain, 0)


def fits(latents, queries, log_decay, w_out, w_up, w_down):
    frames, ranks, pools = (lax.axis_size(a) for a in ("frame", "tensor", "pool"))
    rows, tokens = latents.shape[0], queries.shape[0]
    return (
        frames == 2
        and pools == 4
        and ranks > 1
        and rows % 128 == 0
        and latents.shape[1] % (16 * frames) == 0
        and log_decay.shape[0] < 8
        and rows * ranks == tokens
        and rows % 16 == 0
        and all(w.shape[0] % 16 == 0 and w.shape[0] >= 64 for w in (w_out, w_up, w_down))
        and w_up.shape[0] == w_out.shape[1] == w_down.shape[1]
        and queries.shape[1] // log_decay.shape[0] % 16 == 0
    )


def on_device(
    latents, queries, keys, values, log_decay, block_ids, t_index, w_mod, w_out, w_up, w_down
):
    if not fits(latents, queries, log_decay, w_out, w_up, w_down):
        return by_collectives(
            latents, queries, keys, values, log_decay, block_ids, t_index, w_mod, w_out, w_up, w_down
        )
    ranks, slabs = lax.axis_size("tensor"), lax.axis_size("frame")
    rows, width = latents.shape
    piece = width // slabs
    tokens, features = queries.shape
    head_count = log_decay.shape[0]
    head_size = features // head_count
    time_features, step_size = time_embedding(t_index, w_mod)

    def split(count):
        edges = [count // 16 * i // 4 * 16 for i in range(5)]
        return tuple((edges[i], edges[i + 1] - edges[i]) for i in range(4))

    quarters = tuple(split(w.shape[0]) for w in (w_out, w_up, w_down))
    sizes = (ranks, slabs, head_count, head_size, rows, tokens, quarters)
    block = (ranks, slabs, rows, piece)
    vmem = pl.BlockSpec(memory_space=pltpu.VMEM)
    anywhere = pl.BlockSpec(memory_space=pl.ANY)
    dma = pltpu.SemaphoreType.DMA
    velocity, advanced = pl.pallas_call(
        functools.partial(fused, sizes),
        out_shape=[jax.ShapeDtypeStruct((width, rows), jnp.bfloat16)] * 2,
        in_specs=[vmem] * 8 + [anywhere] * 4,
        out_specs=[vmem] * 2,
        scratch_shapes=[
            pltpu.VMEM((slabs,) + w_out.shape, jnp.bfloat16),
            pltpu.VMEM((slabs,) + w_up.shape, jnp.bfloat16),
            pltpu.VMEM((slabs,) + w_down.shape, jnp.bfloat16),
            pltpu.VMEM(w_mod.shape, jnp.bfloat16),
            pltpu.VMEM((head_count, head_size, head_size), jnp.bfloat16),
            pltpu.VMEM((head_count, head_size, head_size), jnp.bfloat16),
            pltpu.VMEM((tokens, features), jnp.bfloat16),
            pltpu.VMEM(block, jnp.bfloat16),
            pltpu.VMEM((2,) + block, jnp.bfloat16),
            pltpu.VMEM(block, jnp.bfloat16),
            pltpu.VMEM(block, jnp.bfloat16),
            pltpu.VMEM((2,) + block, jnp.bfloat16),
            pltpu.VMEM((slabs, rows, piece), jnp.float32),
            pltpu.VMEM((slabs, rows, piece), jnp.float32),
            pltpu.VMEM((rows, w_up.shape[1]), jnp.bfloat16),
            pltpu.VMEM((8, tokens), jnp.float32),
            pltpu.VMEM((tokens, 8), jnp.float32),
            pltpu.VMEM((head_count, tokens, head_size), jnp.bfloat16),
            pltpu.VMEM((8, w_mod.shape[1]), jnp.float32),
            dma((4,)), dma((3,)), dma((3,)), dma((3,)), dma((3,)), dma((3, 2)), dma((3, 2)), dma((2,)),
            dma((ranks, slabs)), dma((2, ranks, slabs)),
            dma((2, ranks, slabs)), dma((ranks, slabs)),
            dma((ranks, slabs)), dma((2, ranks, slabs)),
        ],
        compiler_params=pltpu.CompilerParams(
            collective_id=0, has_side_effects=True, vmem_limit_bytes=56 * 1024 * 1024
        ),
        name="sublayers",
    )(
        queries.T, keys.T, values.T, log_decay, block_ids[None, :], latents.T,
        jnp.broadcast_to(time_features, (8, time_features.shape[0])), step_size.reshape(1, 1),
        w_out, w_up, w_down, w_mod,
    )
    return (velocity.T, advanced.T)


def solution(mesh):
    return jax.shard_map(
        on_device,
        mesh=mesh,
        in_specs=(
            P(("pool", "frame", "tensor"), None),
            P(("pool", "frame"), "tensor"),
            P(("pool", "frame"), "tensor"),
            P(("pool", "frame"), "tensor"),
            P("tensor", ("pool", "frame")),
            P(("pool", "frame")),
            P("pool"),
            P(),
            P("tensor", "frame"),
            P("frame", "tensor"),
            P("tensor", "frame"),
        ),
        out_specs=(P(("pool", "frame", "tensor"), None), P(("pool", "frame", "tensor"), None)),
        check_vma=False,
    )
```

```python
import functools
import math

import jax
import jax.numpy as jnp
from jax import lax
from jax.experimental import pallas as pl
from jax.experimental.pallas import tpu as pltpu
from jax.sharding import PartitionSpec as P

STEPS = 50


def shifted(block, axis, distance):
    devices = range(lax.axis_size(axis))
    route = [(i - distance, i) for i in devices if i - distance in devices]
    return lax.ppermute(block, axis, route)


def time_embedding(t_index, w_mod):
    fraction = 1.0 - t_index[0].astype(jnp.float32) / STEPS
    following = fraction - 1.0 / STEPS
    sigma_now = 3.0 * fraction / (1.0 + 2.0 * fraction)
    sigma_next = 3.0 * following / (1.0 + 2.0 * following)
    half_width = w_mod.shape[0] // 2
    frequency = jnp.exp(
        -math.log(10000.0) * jnp.arange(half_width).astype(jnp.float32) / half_width
    )
    angles = 1000.0 * sigma_now * frequency
    embedding = jnp.concatenate([jnp.cos(angles), jnp.sin(angles)])
    return (jax.nn.silu(embedding).astype(jnp.bfloat16), sigma_next - sigma_now)


def modulation_of(t_index, w_mod):
    time_features, step_size = time_embedding(t_index, w_mod)
    shifts = jnp.dot(time_features[None, :], w_mod, preferred_element_type=jnp.float32)[0]
    return (shifts, step_size)


def own_state(key_heads, value_heads, cumulative):
    block_total = cumulative[:, -1]
    scaled = key_heads.astype(jnp.float32) * jnp.exp(block_total[:, None] - cumulative)[:, :, None]
    state_sum = jnp.einsum(
        "htd,hte->hde", scaled, value_heads.astype(jnp.float32), precision=lax.Precision.HIGHEST
    )
    return (block_total, state_sum)


def mix_block(query_heads, key_heads, value_heads, cumulative, labels, carried_state):
    factor = query_heads.shape[2] ** (-0.5)
    visible = labels[None, :] <= labels[:, None]
    decay = jnp.exp(jnp.minimum(cumulative[:, :, None] - cumulative[:, None, :], 0.0))
    weights = jnp.where(visible[None], decay, 0.0) * factor
    scores = jnp.einsum("hid,hjd->hij", query_heads, key_heads, preferred_element_type=jnp.float32)
    probs = (scores * weights).astype(jnp.bfloat16)
    inner_part = jnp.einsum("hij,hjd->hid", probs, value_heads, preferred_element_type=jnp.float32)
    carried = jnp.einsum(
        "hid,hde->hie",
        query_heads.astype(jnp.float32),
        carried_state,
        precision=lax.Precision.HIGHEST,
    )
    numerator = inner_part + carried * (jnp.exp(cumulative) * factor)[:, :, None]
    normed = numerator * lax.rsqrt(jnp.mean(numerator * numerator, axis=2, keepdims=True) + 1e-06)
    return normed.astype(jnp.bfloat16)


def layer_norm(hidden):
    centered = hidden - jnp.mean(hidden, axis=1, keepdims=True)
    variance = jnp.mean(centered * centered, axis=1, keepdims=True)
    return centered * lax.rsqrt(variance + 1e-06)


def by_collectives(
    latents, queries, keys, values, log_decay, block_ids, t_index, w_mod, w_out, w_up, w_down
):
    shifts, step_size = modulation_of(t_index, w_mod)
    width = latents.shape[1]
    head_count = log_decay.shape[0]
    token_count = log_decay.shape[1]
    head_size = queries.shape[1] // head_count

    def to_heads(rows_in):
        return rows_in.reshape(token_count, head_count, head_size).transpose(1, 0, 2)

    query_heads = to_heads(queries)
    key_heads = to_heads(keys)
    value_heads = to_heads(values)
    cumulative = jnp.cumsum(log_decay, axis=1)
    block_total, state_sum = own_state(key_heads, value_heads, cumulative)
    keep_factor = jnp.exp(block_total)[:, None, None]

    def relay(turn, incoming):
        return shifted(
            (keep_factor * incoming + state_sum).astype(jnp.bfloat16), "frame", 1
        ).astype(jnp.float32)

    carried_state = lax.fori_loop(0, lax.axis_size("frame") - 1, relay, jnp.zeros_like(state_sum))
    mixed = mix_block(query_heads, key_heads, value_heads, cumulative, block_ids, carried_state)
    mixed_rows = mixed.transpose(1, 0, 2).reshape(token_count, head_count * head_size)
    head_terms = jnp.dot(
        mixed_rows,
        lax.all_gather(w_out, "frame", axis=1, tiled=True),
        preferred_element_type=jnp.float32,
    )
    attention = lax.psum_scatter(
        head_terms.astype(jnp.bfloat16), "tensor", scatter_dimension=0, tiled=True
    ).astype(jnp.float32)
    hidden = latents.astype(jnp.float32) + shifts[3 * width :] * attention
    normed = (layer_norm(hidden) * (1.0 + shifts[width : 2 * width]) + shifts[:width]).astype(
        jnp.bfloat16
    )
    normed_all = lax.all_gather(normed, "tensor", axis=0, tiled=True)
    up_sums = jnp.dot(
        normed_all,
        lax.all_gather(w_up, "frame", axis=0, tiled=True),
        preferred_element_type=jnp.float32,
    )
    units = jax.nn.gelu(up_sums, approximate=True).astype(jnp.bfloat16)
    unit_terms = jnp.dot(
        units,
        lax.all_gather(w_down, "frame", axis=1, tiled=True),
        preferred_element_type=jnp.float32,
    )
    feed = lax.psum_scatter(
        unit_terms.astype(jnp.bfloat16), "tensor", scatter_dimension=0, tiled=True
    ).astype(jnp.float32)
    velocity = (hidden + shifts[2 * width : 3 * width] * feed).astype(jnp.bfloat16)
    advanced = (latents.astype(jnp.float32) + step_size * velocity.astype(jnp.float32)).astype(
        jnp.bfloat16
    )
    return (velocity, advanced)


MESH = pl.DeviceIdType.MESH


def at_most(count, value):
    return jnp.minimum(jnp.maximum(value, 0), count - 1)


def fused(
    sizes,
    q_ref, k_ref, v_ref, decay_ref, label_ref, lat_ref, feature_ref,
    w_out_ref, w_up_ref, w_down_ref, w_mod_ref,
    velocity_ref,
    out_buf, up_buf, down_buf, mod_buf, state_out, state_in, mixed,
    first, first_in, spread, second, second_in, hidden, attended, units_own, columns, down_columns, key_rows, shift_rows,
    own_sem, y_send, y_recv, x_send, x_recv, core_send, core_recv, state_sems,
    first_send, first_recv, spread_send, spread_recv, second_send, second_recv,
):
    ranks, slabs, head_count, head_size, rows, tokens, quarters = sizes
    z = lax.axis_index("tensor")
    f = lax.axis_index("frame")
    pool = lax.axis_index("pool")
    core = lax.rem(pool, 2)
    other_core = pool + 1 - 2 * core
    other_chip = lax.rem(pool + 2, 4)
    other_f = 1 - f
    factor = head_size ** (-0.5)

    barrier = pltpu.get_barrier_semaphore()
    pl.semaphore_signal(barrier, inc=1, device_id={"frame": other_f}, device_id_type=MESH)
    pl.semaphore_signal(barrier, inc=1, device_id={"pool": other_core}, device_id_type=MESH)
    pl.semaphore_signal(barrier, inc=1, device_id={"pool": other_chip}, device_id_type=MESH)

    @pl.when(z > 0)
    def _():
        pl.semaphore_signal(barrier, inc=1, device_id={"tensor": z - 1}, device_id_type=MESH)

    @pl.when(z < ranks - 1)
    def _():
        pl.semaphore_signal(barrier, inc=1, device_id={"tensor": z + 1}, device_id_type=MESH)

    sources = (w_out_ref, w_up_ref, w_down_ref)
    buffers = (out_buf, up_buf, down_buf)
    own_copies = [
        pltpu.make_async_copy(sources[i], buffers[i].at[f], own_sem.at[i]) for i in range(3)
    ]
    for copy in own_copies:
        copy.start()
    mod_copy = pltpu.make_async_copy(w_mod_ref, mod_buf, own_sem.at[3])
    mod_copy.start()

    earlier = (
        lax.broadcasted_iota(jnp.int32, (tokens, tokens), 0)
        <= lax.broadcasted_iota(jnp.int32, (tokens, tokens), 1)
    ).astype(jnp.float32).astype(jnp.bfloat16)
    rest = decay_ref[...]
    cum = jnp.zeros_like(rest)
    for _ in range(3):
        leading = rest.astype(jnp.bfloat16)
        rest = rest - leading.astype(jnp.float32)
        cum += jnp.dot(leading, earlier, preferred_element_type=jnp.float32)
    columns[...] = jnp.zeros_like(columns)
    columns[0:head_count, :] = cum
    columns[head_count : head_count + 1, :] = label_ref[...].astype(jnp.float32)
    down_columns[...] = columns[...].T

    for h in range(head_count):
        part = slice(h * head_size, (h + 1) * head_size)
        row = cum[h : h + 1, :]
        total = row[:, tokens - 1 : tokens]
        keys = k_ref[part, :].astype(jnp.float32)
        key_rows[h] = keys.T.astype(jnp.bfloat16)
        scaled = (keys * jnp.exp(total - row)).astype(jnp.bfloat16)
        state_out[h] = lax.dot_general(
            v_ref[part, :], scaled, (((1,), (1,)), ((), ())), preferred_element_type=jnp.float32
        ).astype(jnp.bfloat16)

    links = 3 + (z > 0).astype(jnp.int32) + (z < ranks - 1).astype(jnp.int32)
    pl.semaphore_wait(barrier, links)

    state_copy = pltpu.make_async_remote_copy(
        src_ref=state_out, dst_ref=state_in, send_sem=state_sems.at[0], recv_sem=state_sems.at[1],
        device_id={"frame": other_f}, device_id_type=MESH,
    )

    @pl.when(f == 0)
    def _():
        state_copy.start()
        state_in[...] = jnp.zeros_like(state_in)

    def across(i, quarter):
        part = pl.ds(*quarters[i][quarter])
        return pltpu.make_async_remote_copy(
            src_ref=sources[i].at[part], dst_ref=buffers[i].at[f, part],
            send_sem=y_send.at[i], recv_sem=y_recv.at[i],
            device_id={"frame": other_f}, device_id_type=MESH,
        )

    def arrived(i, quarter):
        part = pl.ds(*quarters[i][quarter])
        return pltpu.make_async_remote_copy(
            src_ref=sources[i].at[part], dst_ref=buffers[i].at[other_f, part],
            send_sem=y_send.at[i], recv_sem=y_recv.at[i],
            device_id={"frame": other_f}, device_id_type=MESH,
        )

    def region(i, quarter):
        return buffers[i].at[other_f, pl.ds(*quarters[i][quarter])]

    def to_chip(i, quarter):
        return pltpu.make_async_remote_copy(
            src_ref=region(i, quarter), dst_ref=region(i, quarter),
            send_sem=x_send.at[i], recv_sem=x_recv.at[i],
            device_id={"pool": other_chip}, device_id_type=MESH,
        )

    def to_core(i, quarter, turn):
        return pltpu.make_async_remote_copy(
            src_ref=region(i, quarter), dst_ref=region(i, quarter),
            send_sem=core_send.at[i, turn], recv_sem=core_recv.at[i, turn],
            device_id={"pool": other_core}, device_id_type=MESH,
        )

    def each_quarter(act):
        for quarter in range(4):
            @pl.when(pool == quarter)
            def _():
                act(quarter)

    each_quarter(lambda quarter: across(0, quarter).start())

    def pass_on(i):
        def act(quarter):
            arrived(i, quarter).wait_recv()
            to_chip(i, quarter).start()
            to_core(i, quarter, 0).start()
        each_quarter(act)

    def pass_round(i):
        def act(quarter):
            opposite = (quarter + 2) % 4
            to_chip(i, opposite).wait_recv()
            to_core(i, opposite, 1).start()
        each_quarter(act)

    def settle(i):
        def act(quarter):
            to_core(i, quarter ^ 1, 0).wait_recv()
            to_core(i, (quarter ^ 1) ^ 2, 1).wait_recv()
        each_quarter(act)

    @pl.when(f > 0)
    def _():
        state_copy.wait_recv()

    def attend(d):
        block = pl.ds(pl.multiple_of(d * rows, rows), rows)
        visible = (
            down_columns[:, head_count : head_count + 1] <= columns[head_count : head_count + 1, block]
        )
        for h in range(head_count):
            part = slice(h * head_size, (h + 1) * head_size)
            qh = q_ref[part, block]
            scores = jnp.dot(key_rows[h], qh, preferred_element_type=jnp.float32)
            row = columns[h : h + 1, block]
            decay = jnp.exp(jnp.minimum(row - down_columns[:, h : h + 1], 0.0))
            probs = (scores * (jnp.where(visible, decay, 0.0) * factor)).astype(jnp.bfloat16)
            inner = jnp.dot(v_ref[part, :], probs, preferred_element_type=jnp.float32)
            carried = jnp.dot(state_in[h], qh, preferred_element_type=jnp.float32)
            numerator = inner + carried * (jnp.exp(row) * factor)
            power = jnp.mean(numerator * numerator, axis=0, keepdims=True)
            mixed[block, part] = (numerator * lax.rsqrt(power + 1e-06)).T.astype(jnp.bfloat16)

    own_copies[0].wait()

    def rows_of(d):
        return pl.ds(pl.multiple_of(d * rows, rows), rows)

    def hop(buf, landing, send_sem, recv_sem, way, d, s):
        to = at_most(ranks, z + 1 - 2 * way)
        return pltpu.make_async_remote_copy(
            src_ref=buf.at[d, s], dst_ref=landing.at[way, d, s],
            send_sem=send_sem.at[d, s], recv_sem=recv_sem.at[way, d, s],
            device_id={"tensor": to}, device_id_type=MESH,
        )

    def hop1(way, d, s):
        return hop(first, first_in, first_send, first_recv, way, d, s)

    def hop2(way, d, s):
        return hop(second, second_in, second_send, second_recv, way, d, s)

    def has_upstream(way):
        return jnp.where(way == 0, z > 0, z < ranks - 1)

    def first_turn(turn, s, fresh):
        step = turn // 2
        near = jnp.where(z < ranks // 2, 0, 1)
        way = lax.rem(turn + near, 2)
        d = jnp.where(way == 0, ranks - 1 - step, step)
        active = jnp.where(way == 0, d > z, d < z)

        @pl.when(active)
        def _():
            if fresh:
                attend(d)
            part = jnp.dot(mixed[rows_of(d), :], out_buf[s], preferred_element_type=jnp.float32)
            first[d, s] = part.astype(jnp.bfloat16)

            @pl.when(has_upstream(way))
            def _():
                hop1(way, d, s).wait_recv()
                first[d, s] = (
                    first[d, s].astype(jnp.float32) + first_in[way, d, s].astype(jnp.float32)
                ).astype(jnp.bfloat16)

            hop1(way, d, s).start()

    def own_slab(s):
        part = jnp.dot(mixed[rows_of(z), :], out_buf[s], preferred_element_type=jnp.float32)
        attended[s] = part.astype(jnp.bfloat16).astype(jnp.float32)

    def near_columns(turn, carry):
        first_turn(turn, f, True)

        @pl.when(turn == ranks // 2 - 1)
        def _():
            pass_on(0)
            each_quarter(lambda quarter: across(1, quarter).start())

        @pl.when(turn == ranks - 1)
        def _():
            pass_round(0)
            each_quarter(lambda quarter: across(2, quarter).start())

        return carry

    lax.fori_loop(0, 2 * (ranks - 1), near_columns, 0)
    attend(z)
    own_slab(f)
    settle(0)

    def far_columns(turn, carry):
        first_turn(turn, other_f, False)

        @pl.when(turn == 1)
        def _():
            pass_on(1)

        return carry

    lax.fori_loop(0, 2 * (ranks - 1), far_columns, 0)
    own_slab(other_f)

    mod_copy.wait()
    shift_rows[...] = jnp.dot(feature_ref[...], mod_buf[...], preferred_element_type=jnp.float32)
    piece = hidden.shape[2]

    def shift(kind, s):
        start = (kind * slabs + s) * piece
        return shift_rows[0:1, start : start + piece]

    def lat(s):
        return lat_ref[s * piece : (s + 1) * piece, :].astype(jnp.float32).T

    def gather_sums(hop_of, landing, target):
        for way in range(2):
            @pl.when(has_upstream(way))
            def _():
                for s in range(slabs):
                    hop_of(way, z, s).wait_recv()
                    target[s] += landing[way, z, s].astype(jnp.float32)

    gather_sums(hop1, first_in, attended)

    total = jnp.zeros((rows, 1), jnp.float32)
    for s in range(slabs):
        value = lat(s) + shift(3, s) * attended[s]
        hidden[s] = value
        total += jnp.sum(value, axis=1, keepdims=True)
    width = slabs * hidden.shape[2]
    mean = total / width
    squares = jnp.zeros((rows, 1), jnp.float32)
    for s in range(slabs):
        centered = hidden[s] - mean
        squares += jnp.sum(centered * centered, axis=1, keepdims=True)
    inverse = lax.rsqrt(squares / width + 1e-06)
    for s in range(slabs):
        spread[z, s] = (
            (hidden[s] - mean) * inverse * (1.0 + shift(1, s)) + shift(0, s)
        ).astype(jnp.bfloat16)

    def relay(way, c, s):
        to = at_most(ranks, z + 1 - 2 * way)
        return pltpu.make_async_remote_copy(
            src_ref=spread.at[c, s], dst_ref=spread.at[c, s],
            send_sem=spread_send.at[way, c, s], recv_sem=spread_recv.at[c, s],
            device_id={"tensor": to}, device_id_type=MESH,
        )

    def has_downstream(way):
        return jnp.where(way == 0, z < ranks - 1, z > 0)

    for way in range(2):
        @pl.when(has_downstream(way))
        def _():
            for s in range(slabs):
                relay(way, z, s).start()

    pass_round(1)
    pass_on(2)
    own_copies[1].wait()
    settle(1)

    def up_side(c):
        acc = jnp.dot(spread[c, 0], up_buf[0], preferred_element_type=jnp.float32)
        for s in range(1, slabs):
            acc += jnp.dot(spread[c, s], up_buf[s], preferred_element_type=jnp.float32)
        return jax.nn.gelu(acc, approximate=True).astype(jnp.bfloat16)

    units_own[...] = up_side(z)

    def tick(k, carry):
        def chunk_of(way):
            return jnp.where(way == 0, z - k, z + k)

        def arrival(way, c0):
            c = chunk_of(way)

            @pl.when((c >= 0) & (c < ranks))
            def _():
                for s in range(slabs):
                    relay(way, c, s).wait_recv()

                    @pl.when(has_downstream(way))
                    def _():
                        relay(way, c, s).start()

            return c0

        def work(way, c0):
            c = chunk_of(way)

            @pl.when((c >= 0) & (c < ranks))
            def _():
                units = up_side(c)

                @pl.when((k == 1) & ((way == 0) | (z == 0)))
                def _():
                    own_copies[2].wait()
                    pass_round(2)
                    settle(2)

                for s in range(slabs):
                    second[c, s] = jnp.dot(
                        units, down_buf[s], preferred_element_type=jnp.float32
                    ).astype(jnp.bfloat16)

            return c0

        @pl.when(k < ranks)
        def _():
            lax.fori_loop(0, 2, arrival, 0)
            lax.fori_loop(0, 2, work, 0)

        def sending(way, c0):
            place = jnp.where(way == 0, z, ranks - 1 - z)
            ahead = k - place
            d = jnp.where(way == 0, ahead, ranks - 1 - ahead)

            @pl.when((ahead > place) & (ahead < ranks))
            def _():
                def slab(s, c1):
                    @pl.when(has_upstream(way))
                    def _():
                        hop2(way, d, s).wait_recv()
                        second[d, s] = (
                            second[d, s].astype(jnp.float32) + second_in[way, d, s].astype(jnp.float32)
                        ).astype(jnp.bfloat16)

                    hop2(way, d, s).start()
                    return c1

                lax.fori_loop(0, slabs, slab, 0)

            return c0

        lax.fori_loop(0, 2, sending, 0)
        return carry

    lax.fori_loop(1, 2 * ranks - 2, tick, 0)

    for s in range(slabs):
        attended[s] = (
            jnp.dot(units_own[...], down_buf[s], preferred_element_type=jnp.float32)
            .astype(jnp.bfloat16)
            .astype(jnp.float32)
        )
    gather_sums(hop2, second_in, attended)
    for s in range(slabs):
        velocity = hidden[s] + shift(2, s) * attended[s]
        velocity_ref[s * piece : (s + 1) * piece, :] = velocity.T

    @pl.when(f == 0)
    def _():
        state_copy.wait_send()

    for i in range(3):
        def left(quarter):
            across(i, quarter).wait_send()
            to_chip(i, quarter).wait_send()
            to_core(i, quarter, 0).wait_send()
            to_core(i, (quarter + 2) % 4, 1).wait_send()
        each_quarter(left)

    def drain(d, carry):
        def slab(s, c):
            @pl.when(d != z)
            def _():
                way = jnp.where(d > z, 0, 1)
                hop1(way, d, s).wait_send()
                hop2(way, d, s).wait_send()

            def direction(way, c1):
                came = jnp.where(way == 0, d <= z, d >= z)

                @pl.when(came & has_downstream(way))
                def _():
                    relay(way, d, s).wait_send()

                return c1

            lax.fori_loop(0, 2, direction, 0)
            return c

        lax.fori_loop(0, slabs, slab, 0)
        return carry

    lax.fori_loop(0, ranks, drain, 0)


def fits(latents, queries, log_decay, w_out, w_up, w_down):
    frames, ranks, pools = (lax.axis_size(a) for a in ("frame", "tensor", "pool"))
    rows, tokens = latents.shape[0], queries.shape[0]
    return (
        frames == 2
        and pools == 4
        and ranks > 1
        and rows % 128 == 0
        and latents.shape[1] % (16 * frames) == 0
        and log_decay.shape[0] < 8
        and rows * ranks == tokens
        and rows % 16 == 0
        and all(w.shape[0] % 16 == 0 and w.shape[0] >= 64 for w in (w_out, w_up, w_down))
        and w_up.shape[0] == w_out.shape[1] == w_down.shape[1]
        and queries.shape[1] // log_decay.shape[0] % 16 == 0
    )


def on_device(
    latents, queries, keys, values, log_decay, block_ids, t_index, w_mod, w_out, w_up, w_down
):
    if not fits(latents, queries, log_decay, w_out, w_up, w_down):
        return by_collectives(
            latents, queries, keys, values, log_decay, block_ids, t_index, w_mod, w_out, w_up, w_down
        )
    ranks, slabs = lax.axis_size("tensor"), lax.axis_size("frame")
    rows, width = latents.shape
    piece = width // slabs
    tokens, features = queries.shape
    head_count = log_decay.shape[0]
    head_size = features // head_count
    time_features, step_size = time_embedding(t_index, w_mod)

    def split(count):
        edges = [count // 16 * i // 4 * 16 for i in range(5)]
        return tuple((edges[i], edges[i + 1] - edges[i]) for i in range(4))

    quarters = tuple(split(w.shape[0]) for w in (w_out, w_up, w_down))
    sizes = (ranks, slabs, head_count, head_size, rows, tokens, quarters)
    block = (ranks, slabs, rows, piece)
    vmem = pl.BlockSpec(memory_space=pltpu.VMEM)
    anywhere = pl.BlockSpec(memory_space=pl.ANY)
    dma = pltpu.SemaphoreType.DMA
    velocity = pl.pallas_call(
        functools.partial(fused, sizes),
        out_shape=jax.ShapeDtypeStruct((width, rows), jnp.float32),
        in_specs=[vmem] * 7 + [anywhere] * 4,
        out_specs=vmem,
        scratch_shapes=[
            pltpu.VMEM((slabs,) + w_out.shape, jnp.bfloat16),
            pltpu.VMEM((slabs,) + w_up.shape, jnp.bfloat16),
            pltpu.VMEM((slabs,) + w_down.shape, jnp.bfloat16),
            pltpu.VMEM(w_mod.shape, jnp.bfloat16),
            pltpu.VMEM((head_count, head_size, head_size), jnp.bfloat16),
            pltpu.VMEM((head_count, head_size, head_size), jnp.bfloat16),
            pltpu.VMEM((tokens, features), jnp.bfloat16),
            pltpu.VMEM(block, jnp.bfloat16),
            pltpu.VMEM((2,) + block, jnp.bfloat16),
            pltpu.VMEM(block, jnp.bfloat16),
            pltpu.VMEM(block, jnp.bfloat16),
            pltpu.VMEM((2,) + block, jnp.bfloat16),
            pltpu.VMEM((slabs, rows, piece), jnp.float32),
            pltpu.VMEM((slabs, rows, piece), jnp.float32),
            pltpu.VMEM((rows, w_up.shape[1]), jnp.bfloat16),
            pltpu.VMEM((8, tokens), jnp.float32),
            pltpu.VMEM((tokens, 8), jnp.float32),
            pltpu.VMEM((head_count, tokens, head_size), jnp.bfloat16),
            pltpu.VMEM((8, w_mod.shape[1]), jnp.float32),
            dma((4,)), dma((3,)), dma((3,)), dma((3,)), dma((3,)), dma((3, 2)), dma((3, 2)), dma((2,)),
            dma((ranks, slabs)), dma((2, ranks, slabs)),
            dma((2, ranks, slabs)), dma((ranks, slabs)),
            dma((ranks, slabs)), dma((2, ranks, slabs)),
        ],
        compiler_params=pltpu.CompilerParams(
            collective_id=0, has_side_effects=True, vmem_limit_bytes=56 * 1024 * 1024
        ),
        name="sublayers",
    )(
        queries.T, keys.T, values.T, log_decay, block_ids[None, :], latents.T,
        jnp.broadcast_to(time_features, (8, time_features.shape[0])),
        w_out, w_up, w_down, w_mod,
    )
    velocity = velocity.T.astype(jnp.bfloat16)
    advanced = latents.astype(jnp.float32) + step_size * velocity.astype(jnp.float32)
    return (velocity, advanced.astype(jnp.bfloat16))


def solution(mesh):
    return jax.shard_map(
        on_device,
        mesh=mesh,
        in_specs=(
            P(("pool", "frame", "tensor"), None),
            P(("pool", "frame"), "tensor"),
            P(("pool", "frame"), "tensor"),
            P(("pool", "frame"), "tensor"),
            P("tensor", ("pool", "frame")),
            P(("pool", "frame")),
            P("pool"),
            P(),
            P("tensor", "frame"),
            P("frame", "tensor"),
            P("tensor", "frame"),
        ),
        out_specs=(P(("pool", "frame", "tensor"), None), P(("pool", "frame", "tensor"), None)),
        check_vma=False,
    )
```

```python
import functools
import math

import jax
import jax.numpy as jnp
from jax import lax
from jax.experimental import pallas as pl
from jax.experimental.pallas import tpu as pltpu
from jax.sharding import PartitionSpec as P

STEPS = 50


def shifted(block, axis, distance):
    devices = range(lax.axis_size(axis))
    route = [(i - distance, i) for i in devices if i - distance in devices]
    return lax.ppermute(block, axis, route)


def time_embedding(t_index, w_mod):
    fraction = 1.0 - t_index[0].astype(jnp.float32) / STEPS
    following = fraction - 1.0 / STEPS
    sigma_now = 3.0 * fraction / (1.0 + 2.0 * fraction)
    sigma_next = 3.0 * following / (1.0 + 2.0 * following)
    half_width = w_mod.shape[0] // 2
    frequency = jnp.exp(
        -math.log(10000.0) * jnp.arange(half_width).astype(jnp.float32) / half_width
    )
    angles = 1000.0 * sigma_now * frequency
    embedding = jnp.concatenate([jnp.cos(angles), jnp.sin(angles)])
    return (jax.nn.silu(embedding).astype(jnp.bfloat16), sigma_next - sigma_now)


def modulation_of(t_index, w_mod):
    time_features, step_size = time_embedding(t_index, w_mod)
    shifts = jnp.dot(time_features[None, :], w_mod, preferred_element_type=jnp.float32)[0]
    return (shifts, step_size)


def own_state(key_heads, value_heads, cumulative):
    block_total = cumulative[:, -1]
    scaled = key_heads.astype(jnp.float32) * jnp.exp(block_total[:, None] - cumulative)[:, :, None]
    state_sum = jnp.einsum(
        "htd,hte->hde", scaled, value_heads.astype(jnp.float32), precision=lax.Precision.HIGHEST
    )
    return (block_total, state_sum)


def mix_block(query_heads, key_heads, value_heads, cumulative, labels, carried_state):
    factor = query_heads.shape[2] ** (-0.5)
    visible = labels[None, :] <= labels[:, None]
    decay = jnp.exp(jnp.minimum(cumulative[:, :, None] - cumulative[:, None, :], 0.0))
    weights = jnp.where(visible[None], decay, 0.0) * factor
    scores = jnp.einsum("hid,hjd->hij", query_heads, key_heads, preferred_element_type=jnp.float32)
    probs = (scores * weights).astype(jnp.bfloat16)
    inner_part = jnp.einsum("hij,hjd->hid", probs, value_heads, preferred_element_type=jnp.float32)
    carried = jnp.einsum(
        "hid,hde->hie",
        query_heads.astype(jnp.float32),
        carried_state,
        precision=lax.Precision.HIGHEST,
    )
    numerator = inner_part + carried * (jnp.exp(cumulative) * factor)[:, :, None]
    normed = numerator * lax.rsqrt(jnp.mean(numerator * numerator, axis=2, keepdims=True) + 1e-06)
    return normed.astype(jnp.bfloat16)


def layer_norm(hidden):
    centered = hidden - jnp.mean(hidden, axis=1, keepdims=True)
    variance = jnp.mean(centered * centered, axis=1, keepdims=True)
    return centered * lax.rsqrt(variance + 1e-06)


def by_collectives(
    latents, queries, keys, values, log_decay, block_ids, t_index, w_mod, w_out, w_up, w_down
):
    shifts, step_size = modulation_of(t_index, w_mod)
    width = latents.shape[1]
    head_count = log_decay.shape[0]
    token_count = log_decay.shape[1]
    head_size = queries.shape[1] // head_count

    def to_heads(rows_in):
        return rows_in.reshape(token_count, head_count, head_size).transpose(1, 0, 2)

    query_heads = to_heads(queries)
    key_heads = to_heads(keys)
    value_heads = to_heads(values)
    cumulative = jnp.cumsum(log_decay, axis=1)
    block_total, state_sum = own_state(key_heads, value_heads, cumulative)
    keep_factor = jnp.exp(block_total)[:, None, None]

    def relay(turn, incoming):
        return shifted(
            (keep_factor * incoming + state_sum).astype(jnp.bfloat16), "frame", 1
        ).astype(jnp.float32)

    carried_state = lax.fori_loop(0, lax.axis_size("frame") - 1, relay, jnp.zeros_like(state_sum))
    mixed = mix_block(query_heads, key_heads, value_heads, cumulative, block_ids, carried_state)
    mixed_rows = mixed.transpose(1, 0, 2).reshape(token_count, head_count * head_size)
    head_terms = jnp.dot(
        mixed_rows,
        lax.all_gather(w_out, "frame", axis=1, tiled=True),
        preferred_element_type=jnp.float32,
    )
    attention = lax.psum_scatter(
        head_terms.astype(jnp.bfloat16), "tensor", scatter_dimension=0, tiled=True
    ).astype(jnp.float32)
    hidden = latents.astype(jnp.float32) + shifts[3 * width :] * attention
    normed = (layer_norm(hidden) * (1.0 + shifts[width : 2 * width]) + shifts[:width]).astype(
        jnp.bfloat16
    )
    normed_all = lax.all_gather(normed, "tensor", axis=0, tiled=True)
    up_sums = jnp.dot(
        normed_all,
        lax.all_gather(w_up, "frame", axis=0, tiled=True),
        preferred_element_type=jnp.float32,
    )
    units = jax.nn.gelu(up_sums, approximate=True).astype(jnp.bfloat16)
    unit_terms = jnp.dot(
        units,
        lax.all_gather(w_down, "frame", axis=1, tiled=True),
        preferred_element_type=jnp.float32,
    )
    feed = lax.psum_scatter(
        unit_terms.astype(jnp.bfloat16), "tensor", scatter_dimension=0, tiled=True
    ).astype(jnp.float32)
    velocity = (hidden + shifts[2 * width : 3 * width] * feed).astype(jnp.bfloat16)
    advanced = (latents.astype(jnp.float32) + step_size * velocity.astype(jnp.float32)).astype(
        jnp.bfloat16
    )
    return (velocity, advanced)


MESH = pl.DeviceIdType.MESH


def at_most(count, value):
    return jnp.minimum(jnp.maximum(value, 0), count - 1)


def fused(
    sizes,
    q_ref, k_ref, v_ref, decay_ref, label_ref, lat_ref, feature_ref,
    w_out_ref, w_up_ref, w_down_ref, w_mod_ref,
    velocity_ref,
    out_buf, up_buf, down_buf, mod_buf, state_out, state_in, mixed,
    first, first_in, spread, second, second_in, hidden, attended, units_own, columns, down_columns, key_rows, shift_rows,
    own_sem, y_send, y_recv, x_send, x_recv, core_send, core_recv, state_sems,
    first_send, first_recv, spread_send, spread_recv, second_send, second_recv,
):
    ranks, slabs, head_count, head_size, rows, tokens, quarters = sizes
    z = lax.axis_index("tensor")
    f = lax.axis_index("frame")
    pool = lax.axis_index("pool")
    core = lax.rem(pool, 2)
    other_core = pool + 1 - 2 * core
    other_chip = lax.rem(pool + 2, 4)
    other_f = 1 - f
    factor = head_size ** (-0.5)

    barrier = pltpu.get_barrier_semaphore()
    pl.semaphore_signal(barrier, inc=1, device_id={"frame": other_f}, device_id_type=MESH)
    pl.semaphore_signal(barrier, inc=1, device_id={"pool": other_core}, device_id_type=MESH)
    pl.semaphore_signal(barrier, inc=1, device_id={"pool": other_chip}, device_id_type=MESH)

    @pl.when(z > 0)
    def _():
        pl.semaphore_signal(barrier, inc=1, device_id={"tensor": z - 1}, device_id_type=MESH)

    @pl.when(z < ranks - 1)
    def _():
        pl.semaphore_signal(barrier, inc=1, device_id={"tensor": z + 1}, device_id_type=MESH)

    sources = (w_out_ref, w_up_ref, w_down_ref)
    buffers = (out_buf, up_buf, down_buf)
    own_copies = [
        pltpu.make_async_copy(sources[i], buffers[i].at[f], own_sem.at[i]) for i in range(3)
    ]
    for copy in own_copies:
        copy.start()
    mod_copy = pltpu.make_async_copy(w_mod_ref, mod_buf, own_sem.at[3])
    mod_copy.start()

    earlier = (
        lax.broadcasted_iota(jnp.int32, (tokens, tokens), 0)
        <= lax.broadcasted_iota(jnp.int32, (tokens, tokens), 1)
    ).astype(jnp.float32).astype(jnp.bfloat16)
    rest = decay_ref[...]
    cum = jnp.zeros_like(rest)
    for _ in range(3):
        leading = rest.astype(jnp.bfloat16)
        rest = rest - leading.astype(jnp.float32)
        cum += jnp.dot(leading, earlier, preferred_element_type=jnp.float32)
    columns[...] = jnp.zeros_like(columns)
    columns[0:head_count, :] = cum
    columns[head_count : head_count + 1, :] = label_ref[...].astype(jnp.float32)
    down_columns[...] = columns[...].T

    for h in range(head_count):
        part = slice(h * head_size, (h + 1) * head_size)
        row = cum[h : h + 1, :]
        total = row[:, tokens - 1 : tokens]
        keys = k_ref[part, :].astype(jnp.float32)
        key_rows[h] = keys.T.astype(jnp.bfloat16)
        scaled = (keys * jnp.exp(total - row)).astype(jnp.bfloat16)
        state_out[h] = lax.dot_general(
            v_ref[part, :], scaled, (((1,), (1,)), ((), ())), preferred_element_type=jnp.float32
        ).astype(jnp.bfloat16)

    links = 3 + (z > 0).astype(jnp.int32) + (z < ranks - 1).astype(jnp.int32)
    pl.semaphore_wait(barrier, links)

    state_copy = pltpu.make_async_remote_copy(
        src_ref=state_out, dst_ref=state_in, send_sem=state_sems.at[0], recv_sem=state_sems.at[1],
        device_id={"frame": other_f}, device_id_type=MESH,
    )

    @pl.when(f == 0)
    def _():
        state_copy.start()
        state_in[...] = jnp.zeros_like(state_in)

    def across(i, quarter):
        part = pl.ds(*quarters[i][quarter])
        return pltpu.make_async_remote_copy(
            src_ref=sources[i].at[part], dst_ref=buffers[i].at[f, part],
            send_sem=y_send.at[i], recv_sem=y_recv.at[i],
            device_id={"frame": other_f}, device_id_type=MESH,
        )

    def arrived(i, quarter):
        part = pl.ds(*quarters[i][quarter])
        return pltpu.make_async_remote_copy(
            src_ref=sources[i].at[part], dst_ref=buffers[i].at[other_f, part],
            send_sem=y_send.at[i], recv_sem=y_recv.at[i],
            device_id={"frame": other_f}, device_id_type=MESH,
        )

    def region(i, quarter):
        return buffers[i].at[other_f, pl.ds(*quarters[i][quarter])]

    def to_chip(i, quarter):
        return pltpu.make_async_remote_copy(
            src_ref=region(i, quarter), dst_ref=region(i, quarter),
            send_sem=x_send.at[i], recv_sem=x_recv.at[i],
            device_id={"pool": other_chip}, device_id_type=MESH,
        )

    def to_core(i, quarter, turn):
        return pltpu.make_async_remote_copy(
            src_ref=region(i, quarter), dst_ref=region(i, quarter),
            send_sem=core_send.at[i, turn], recv_sem=core_recv.at[i, turn],
            device_id={"pool": other_core}, device_id_type=MESH,
        )

    def each_quarter(act):
        for quarter in range(4):
            @pl.when(pool == quarter)
            def _():
                act(quarter)

    each_quarter(lambda quarter: across(0, quarter).start())

    def pass_on(i):
        def act(quarter):
            arrived(i, quarter).wait_recv()
            to_chip(i, quarter).start()
            to_core(i, quarter, 0).start()
        each_quarter(act)

    def pass_round(i):
        def act(quarter):
            opposite = (quarter + 2) % 4
            to_chip(i, opposite).wait_recv()
            to_core(i, opposite, 1).start()
        each_quarter(act)

    def settle(i):
        def act(quarter):
            to_core(i, quarter ^ 1, 0).wait_recv()
            to_core(i, (quarter ^ 1) ^ 2, 1).wait_recv()
        each_quarter(act)

    @pl.when(f > 0)
    def _():
        state_copy.wait_recv()

    def attend(d):
        block = pl.ds(pl.multiple_of(d * rows, rows), rows)
        visible = (
            down_columns[:, head_count : head_count + 1] <= columns[head_count : head_count + 1, block]
        )
        for h in range(head_count):
            part = slice(h * head_size, (h + 1) * head_size)
            qh = q_ref[part, block]
            scores = jnp.dot(key_rows[h], qh, preferred_element_type=jnp.float32)
            row = columns[h : h + 1, block]
            decay = jnp.exp(jnp.minimum(row - down_columns[:, h : h + 1], 0.0))
            probs = (scores * (jnp.where(visible, decay, 0.0) * factor)).astype(jnp.bfloat16)
            inner = jnp.dot(v_ref[part, :], probs, preferred_element_type=jnp.float32)
            carried = jnp.dot(state_in[h], qh, preferred_element_type=jnp.float32)
            numerator = inner + carried * (jnp.exp(row) * factor)
            power = jnp.mean(numerator * numerator, axis=0, keepdims=True)
            mixed[block, part] = (numerator * lax.rsqrt(power + 1e-06)).T.astype(jnp.bfloat16)

    own_copies[0].wait()

    def rows_of(d):
        return pl.ds(pl.multiple_of(d * rows, rows), rows)

    def hop(buf, landing, send_sem, recv_sem, way, d, s):
        to = at_most(ranks, z + 1 - 2 * way)
        return pltpu.make_async_remote_copy(
            src_ref=buf.at[d, s], dst_ref=landing.at[way, d, s],
            send_sem=send_sem.at[d, s], recv_sem=recv_sem.at[way, d, s],
            device_id={"tensor": to}, device_id_type=MESH,
        )

    def hop1(way, d, s):
        return hop(first, first_in, first_send, first_recv, way, d, s)

    shares = second_send.shape[2]

    def share(r):
        return pl.ds(r * (rows // shares), rows // shares)

    def hop2(way, d, s, r):
        to = at_most(ranks, z + 1 - 2 * way)
        return pltpu.make_async_remote_copy(
            src_ref=second.at[d, s, share(r)], dst_ref=second_in.at[way, d, s, share(r)],
            send_sem=second_send.at[d, s, r], recv_sem=second_recv.at[way, d, s, r],
            device_id={"tensor": to}, device_id_type=MESH,
        )

    def has_upstream(way):
        return jnp.where(way == 0, z > 0, z < ranks - 1)

    def first_turn(turn, s, fresh):
        step = turn // 2
        near = jnp.where(z < ranks // 2, 0, 1)
        way = lax.rem(turn + near, 2)
        d = jnp.where(way == 0, ranks - 1 - step, step)
        active = jnp.where(way == 0, d > z, d < z)

        @pl.when(active)
        def _():
            if fresh:
                attend(d)
            part = jnp.dot(mixed[rows_of(d), :], out_buf[s], preferred_element_type=jnp.float32)
            first[d, s] = part.astype(jnp.bfloat16)

            @pl.when(has_upstream(way))
            def _():
                hop1(way, d, s).wait_recv()
                first[d, s] = (
                    first[d, s].astype(jnp.float32) + first_in[way, d, s].astype(jnp.float32)
                ).astype(jnp.bfloat16)

            hop1(way, d, s).start()

    def own_slab(s):
        part = jnp.dot(mixed[rows_of(z), :], out_buf[s], preferred_element_type=jnp.float32)
        attended[s] = part.astype(jnp.bfloat16).astype(jnp.float32)

    def near_columns(turn, carry):
        first_turn(turn, f, True)

        @pl.when(turn == ranks // 2 - 1)
        def _():
            pass_on(0)
            each_quarter(lambda quarter: across(1, quarter).start())

        @pl.when(turn == ranks - 1)
        def _():
            pass_round(0)
            each_quarter(lambda quarter: across(2, quarter).start())

        return carry

    lax.fori_loop(0, 2 * (ranks - 1), near_columns, 0)
    attend(z)
    own_slab(f)
    settle(0)

    def far_columns(turn, carry):
        first_turn(turn, other_f, False)

        @pl.when(turn == 1)
        def _():
            pass_on(1)

        return carry

    lax.fori_loop(0, 2 * (ranks - 1), far_columns, 0)
    own_slab(other_f)

    mod_copy.wait()
    shift_rows[...] = jnp.dot(feature_ref[...], mod_buf[...], preferred_element_type=jnp.float32)
    piece = hidden.shape[2]

    def shift(kind, s):
        start = (kind * slabs + s) * piece
        return shift_rows[0:1, start : start + piece]

    def lat(s):
        return lat_ref[s * piece : (s + 1) * piece, :].astype(jnp.float32).T

    for way in range(2):
        @pl.when(has_upstream(way))
        def _():
            for s in range(slabs):
                hop1(way, z, s).wait_recv()
                attended[s] += first_in[way, z, s].astype(jnp.float32)

    total = jnp.zeros((rows, 1), jnp.float32)
    for s in range(slabs):
        value = lat(s) + shift(3, s) * attended[s]
        hidden[s] = value
        total += jnp.sum(value, axis=1, keepdims=True)
    width = slabs * hidden.shape[2]
    mean = total / width
    squares = jnp.zeros((rows, 1), jnp.float32)
    for s in range(slabs):
        centered = hidden[s] - mean
        squares += jnp.sum(centered * centered, axis=1, keepdims=True)
    inverse = lax.rsqrt(squares / width + 1e-06)
    for s in range(slabs):
        spread[z, s] = (
            (hidden[s] - mean) * inverse * (1.0 + shift(1, s)) + shift(0, s)
        ).astype(jnp.bfloat16)

    def relay(way, c, s):
        to = at_most(ranks, z + 1 - 2 * way)
        return pltpu.make_async_remote_copy(
            src_ref=spread.at[c, s], dst_ref=spread.at[c, s],
            send_sem=spread_send.at[way, c, s], recv_sem=spread_recv.at[c, s],
            device_id={"tensor": to}, device_id_type=MESH,
        )

    def has_downstream(way):
        return jnp.where(way == 0, z < ranks - 1, z > 0)

    for way in range(2):
        @pl.when(has_downstream(way))
        def _():
            for s in range(slabs):
                relay(way, z, s).start()

    pass_round(1)
    pass_on(2)
    own_copies[1].wait()
    settle(1)

    def up_side(c):
        acc = jnp.dot(spread[c, 0], up_buf[0], preferred_element_type=jnp.float32)
        for s in range(1, slabs):
            acc += jnp.dot(spread[c, s], up_buf[s], preferred_element_type=jnp.float32)
        return jax.nn.gelu(acc, approximate=True).astype(jnp.bfloat16)

    units_own[...] = up_side(z)

    def tick(k, carry):
        def chunk_of(way):
            return jnp.where(way == 0, z - k, z + k)

        def arrival(way, c0):
            c = chunk_of(way)

            @pl.when((c >= 0) & (c < ranks))
            def _():
                for s in range(slabs):
                    relay(way, c, s).wait_recv()

                    @pl.when(has_downstream(way))
                    def _():
                        relay(way, c, s).start()

            return c0

        def work(way, c0):
            c = chunk_of(way)

            @pl.when((c >= 0) & (c < ranks))
            def _():
                units = up_side(c)

                @pl.when((k == 1) & ((way == 0) | (z == 0)))
                def _():
                    own_copies[2].wait()
                    pass_round(2)
                    settle(2)

                for s in range(slabs):
                    second[c, s] = jnp.dot(
                        units, down_buf[s], preferred_element_type=jnp.float32
                    ).astype(jnp.bfloat16)

                    @pl.when(jnp.logical_not(has_upstream(1 - way)))
                    def _():
                        for r in range(shares):
                            hop2(1 - way, c, s, r).start()

            return c0

        @pl.when(k < ranks)
        def _():
            lax.fori_loop(0, 2, arrival, 0)
            lax.fori_loop(0, 2, work, 0)

        def sending(way, c0):
            place = jnp.where(way == 0, z, ranks - 1 - z)
            ahead = k - place
            d = jnp.where(way == 0, ahead, ranks - 1 - ahead)

            @pl.when((place > 0) & (ahead > place) & (ahead < ranks))
            def _():
                def slab(s, c1):
                    for r in range(shares):
                        hop2(way, d, s, r).wait_recv()
                        second[d, s, share(r)] = (
                            second[d, s, share(r)].astype(jnp.float32)
                            + second_in[way, d, s, share(r)].astype(jnp.float32)
                        ).astype(jnp.bfloat16)
                        hop2(way, d, s, r).start()
                    return c1

                lax.fori_loop(0, slabs, slab, 0)

            return c0

        lax.fori_loop(0, 2, sending, 0)
        return carry

    lax.fori_loop(1, 2 * ranks - 2, tick, 0)

    for s in range(slabs):
        attended[s] = (
            jnp.dot(units_own[...], down_buf[s], preferred_element_type=jnp.float32)
            .astype(jnp.bfloat16)
            .astype(jnp.float32)
        )
    for way in range(2):
        @pl.when(has_upstream(way))
        def _():
            for s in range(slabs):
                for r in range(shares):
                    hop2(way, z, s, r).wait_recv()
                attended[s] += second_in[way, z, s].astype(jnp.float32)
    for s in range(slabs):
        velocity = hidden[s] + shift(2, s) * attended[s]
        velocity_ref[s * piece : (s + 1) * piece, :] = velocity.T

    @pl.when(f == 0)
    def _():
        state_copy.wait_send()

    for i in range(3):
        def left(quarter):
            across(i, quarter).wait_send()
            to_chip(i, quarter).wait_send()
            to_core(i, quarter, 0).wait_send()
            to_core(i, (quarter + 2) % 4, 1).wait_send()
        each_quarter(left)

    def drain(d, carry):
        def slab(s, c):
            @pl.when(d != z)
            def _():
                way = jnp.where(d > z, 0, 1)
                hop1(way, d, s).wait_send()
                for r in range(shares):
                    hop2(way, d, s, r).wait_send()

            def direction(way, c1):
                came = jnp.where(way == 0, d <= z, d >= z)

                @pl.when(came & has_downstream(way))
                def _():
                    relay(way, d, s).wait_send()

                return c1

            lax.fori_loop(0, 2, direction, 0)
            return c

        lax.fori_loop(0, slabs, slab, 0)
        return carry

    lax.fori_loop(0, ranks, drain, 0)


def fits(latents, queries, log_decay, w_out, w_up, w_down):
    frames, ranks, pools = (lax.axis_size(a) for a in ("frame", "tensor", "pool"))
    rows, tokens = latents.shape[0], queries.shape[0]
    return (
        frames == 2
        and pools == 4
        and ranks > 1
        and rows % 128 == 0
        and latents.shape[1] % (16 * frames) == 0
        and log_decay.shape[0] < 8
        and rows * ranks == tokens
        and rows % 16 == 0
        and all(w.shape[0] % 16 == 0 and w.shape[0] >= 64 for w in (w_out, w_up, w_down))
        and w_up.shape[0] == w_out.shape[1] == w_down.shape[1]
        and queries.shape[1] // log_decay.shape[0] % 16 == 0
    )


def on_device(
    latents, queries, keys, values, log_decay, block_ids, t_index, w_mod, w_out, w_up, w_down
):
    if not fits(latents, queries, log_decay, w_out, w_up, w_down):
        return by_collectives(
            latents, queries, keys, values, log_decay, block_ids, t_index, w_mod, w_out, w_up, w_down
        )
    ranks, slabs = lax.axis_size("tensor"), lax.axis_size("frame")
    rows, width = latents.shape
    piece = width // slabs
    tokens, features = queries.shape
    head_count = log_decay.shape[0]
    head_size = features // head_count
    time_features, step_size = time_embedding(t_index, w_mod)

    def split(count):
        edges = [count // 16 * i // 4 * 16 for i in range(5)]
        return tuple((edges[i], edges[i + 1] - edges[i]) for i in range(4))

    quarters = tuple(split(w.shape[0]) for w in (w_out, w_up, w_down))
    sizes = (ranks, slabs, head_count, head_size, rows, tokens, quarters)
    block = (ranks, slabs, rows, piece)
    vmem = pl.BlockSpec(memory_space=pltpu.VMEM)
    anywhere = pl.BlockSpec(memory_space=pl.ANY)
    dma = pltpu.SemaphoreType.DMA
    velocity = pl.pallas_call(
        functools.partial(fused, sizes),
        out_shape=jax.ShapeDtypeStruct((width, rows), jnp.float32),
        in_specs=[vmem] * 7 + [anywhere] * 4,
        out_specs=vmem,
        scratch_shapes=[
            pltpu.VMEM((slabs,) + w_out.shape, jnp.bfloat16),
            pltpu.VMEM((slabs,) + w_up.shape, jnp.bfloat16),
            pltpu.VMEM((slabs,) + w_down.shape, jnp.bfloat16),
            pltpu.VMEM(w_mod.shape, jnp.bfloat16),
            pltpu.VMEM((head_count, head_size, head_size), jnp.bfloat16),
            pltpu.VMEM((head_count, head_size, head_size), jnp.bfloat16),
            pltpu.VMEM((tokens, features), jnp.bfloat16),
            pltpu.VMEM(block, jnp.bfloat16),
            pltpu.VMEM((2,) + block, jnp.bfloat16),
            pltpu.VMEM(block, jnp.bfloat16),
            pltpu.VMEM(block, jnp.bfloat16),
            pltpu.VMEM((2,) + block, jnp.bfloat16),
            pltpu.VMEM((slabs, rows, piece), jnp.float32),
            pltpu.VMEM((slabs, rows, piece), jnp.float32),
            pltpu.VMEM((rows, w_up.shape[1]), jnp.bfloat16),
            pltpu.VMEM((8, tokens), jnp.float32),
            pltpu.VMEM((tokens, 8), jnp.float32),
            pltpu.VMEM((head_count, tokens, head_size), jnp.bfloat16),
            pltpu.VMEM((8, w_mod.shape[1]), jnp.float32),
            dma((4,)), dma((3,)), dma((3,)), dma((3,)), dma((3,)), dma((3, 2)), dma((3, 2)), dma((2,)),
            dma((ranks, slabs)), dma((2, ranks, slabs)),
            dma((2, ranks, slabs)), dma((ranks, slabs)),
            dma((ranks, slabs, 4)), dma((2, ranks, slabs, 4)),
        ],
        compiler_params=pltpu.CompilerParams(
            collective_id=0, has_side_effects=True, vmem_limit_bytes=56 * 1024 * 1024
        ),
        name="sublayers",
    )(
        queries.T, keys.T, values.T, log_decay, block_ids[None, :], latents.T,
        jnp.broadcast_to(time_features, (8, time_features.shape[0])),
        w_out, w_up, w_down, w_mod,
    )
    velocity = velocity.T.astype(jnp.bfloat16)
    advanced = latents.astype(jnp.float32) + step_size * velocity.astype(jnp.float32)
    return (velocity, advanced.astype(jnp.bfloat16))


def solution(mesh):
    return jax.shard_map(
        on_device,
        mesh=mesh,
        in_specs=(
            P(("pool", "frame", "tensor"), None),
            P(("pool", "frame"), "tensor"),
            P(("pool", "frame"), "tensor"),
            P(("pool", "frame"), "tensor"),
            P("tensor", ("pool", "frame")),
            P(("pool", "frame")),
            P("pool"),
            P(),
            P("tensor", "frame"),
            P("frame", "tensor"),
            P("tensor", "frame"),
        ),
        out_specs=(P(("pool", "frame", "tensor"), None), P(("pool", "frame", "tensor"), None)),
        check_vma=False,
    )
```

```python
import functools
import math

import jax
import jax.numpy as jnp
from jax import lax
from jax.experimental import pallas as pl
from jax.experimental.pallas import tpu as pltpu
from jax.sharding import PartitionSpec as P

STEPS = 50


def shifted(block, axis, distance):
    devices = range(lax.axis_size(axis))
    route = [(i - distance, i) for i in devices if i - distance in devices]
    return lax.ppermute(block, axis, route)


def time_embedding(t_index, w_mod):
    fraction = 1.0 - t_index[0].astype(jnp.float32) / STEPS
    following = fraction - 1.0 / STEPS
    sigma_now = 3.0 * fraction / (1.0 + 2.0 * fraction)
    sigma_next = 3.0 * following / (1.0 + 2.0 * following)
    half_width = w_mod.shape[0] // 2
    frequency = jnp.exp(
        -math.log(10000.0) * jnp.arange(half_width).astype(jnp.float32) / half_width
    )
    angles = 1000.0 * sigma_now * frequency
    embedding = jnp.concatenate([jnp.cos(angles), jnp.sin(angles)])
    return (jax.nn.silu(embedding).astype(jnp.bfloat16), sigma_next - sigma_now)


def modulation_of(t_index, w_mod):
    time_features, step_size = time_embedding(t_index, w_mod)
    shifts = jnp.dot(time_features[None, :], w_mod, preferred_element_type=jnp.float32)[0]
    return (shifts, step_size)


def own_state(key_heads, value_heads, cumulative):
    block_total = cumulative[:, -1]
    scaled = key_heads.astype(jnp.float32) * jnp.exp(block_total[:, None] - cumulative)[:, :, None]
    state_sum = jnp.einsum(
        "htd,hte->hde", scaled, value_heads.astype(jnp.float32), precision=lax.Precision.HIGHEST
    )
    return (block_total, state_sum)


def mix_block(query_heads, key_heads, value_heads, cumulative, labels, carried_state):
    factor = query_heads.shape[2] ** (-0.5)
    visible = labels[None, :] <= labels[:, None]
    decay = jnp.exp(jnp.minimum(cumulative[:, :, None] - cumulative[:, None, :], 0.0))
    weights = jnp.where(visible[None], decay, 0.0) * factor
    scores = jnp.einsum("hid,hjd->hij", query_heads, key_heads, preferred_element_type=jnp.float32)
    probs = (scores * weights).astype(jnp.bfloat16)
    inner_part = jnp.einsum("hij,hjd->hid", probs, value_heads, preferred_element_type=jnp.float32)
    carried = jnp.einsum(
        "hid,hde->hie",
        query_heads.astype(jnp.float32),
        carried_state,
        precision=lax.Precision.HIGHEST,
    )
    numerator = inner_part + carried * (jnp.exp(cumulative) * factor)[:, :, None]
    normed = numerator * lax.rsqrt(jnp.mean(numerator * numerator, axis=2, keepdims=True) + 1e-06)
    return normed.astype(jnp.bfloat16)


def layer_norm(hidden):
    centered = hidden - jnp.mean(hidden, axis=1, keepdims=True)
    variance = jnp.mean(centered * centered, axis=1, keepdims=True)
    return centered * lax.rsqrt(variance + 1e-06)


def by_collectives(
    latents, queries, keys, values, log_decay, block_ids, t_index, w_mod, w_out, w_up, w_down
):
    shifts, step_size = modulation_of(t_index, w_mod)
    width = latents.shape[1]
    head_count = log_decay.shape[0]
    token_count = log_decay.shape[1]
    head_size = queries.shape[1] // head_count

    def to_heads(rows_in):
        return rows_in.reshape(token_count, head_count, head_size).transpose(1, 0, 2)

    query_heads = to_heads(queries)
    key_heads = to_heads(keys)
    value_heads = to_heads(values)
    cumulative = jnp.cumsum(log_decay, axis=1)
    block_total, state_sum = own_state(key_heads, value_heads, cumulative)
    keep_factor = jnp.exp(block_total)[:, None, None]

    def relay(turn, incoming):
        return shifted(
            (keep_factor * incoming + state_sum).astype(jnp.bfloat16), "frame", 1
        ).astype(jnp.float32)

    carried_state = lax.fori_loop(0, lax.axis_size("frame") - 1, relay, jnp.zeros_like(state_sum))
    mixed = mix_block(query_heads, key_heads, value_heads, cumulative, block_ids, carried_state)
    mixed_rows = mixed.transpose(1, 0, 2).reshape(token_count, head_count * head_size)
    head_terms = jnp.dot(
        mixed_rows,
        lax.all_gather(w_out, "frame", axis=1, tiled=True),
        preferred_element_type=jnp.float32,
    )
    attention = lax.psum_scatter(
        head_terms.astype(jnp.bfloat16), "tensor", scatter_dimension=0, tiled=True
    ).astype(jnp.float32)
    hidden = latents.astype(jnp.float32) + shifts[3 * width :] * attention
    normed = (layer_norm(hidden) * (1.0 + shifts[width : 2 * width]) + shifts[:width]).astype(
        jnp.bfloat16
    )
    normed_all = lax.all_gather(normed, "tensor", axis=0, tiled=True)
    up_sums = jnp.dot(
        normed_all,
        lax.all_gather(w_up, "frame", axis=0, tiled=True),
        preferred_element_type=jnp.float32,
    )
    units = jax.nn.gelu(up_sums, approximate=True).astype(jnp.bfloat16)
    unit_terms = jnp.dot(
        units,
        lax.all_gather(w_down, "frame", axis=1, tiled=True),
        preferred_element_type=jnp.float32,
    )
    feed = lax.psum_scatter(
        unit_terms.astype(jnp.bfloat16), "tensor", scatter_dimension=0, tiled=True
    ).astype(jnp.float32)
    velocity = (hidden + shifts[2 * width : 3 * width] * feed).astype(jnp.bfloat16)
    advanced = (latents.astype(jnp.float32) + step_size * velocity.astype(jnp.float32)).astype(
        jnp.bfloat16
    )
    return (velocity, advanced)


MESH = pl.DeviceIdType.MESH


def at_most(count, value):
    return jnp.minimum(jnp.maximum(value, 0), count - 1)


def fused(
    sizes,
    q_ref, k_ref, v_ref, decay_ref, label_ref, lat_ref, feature_ref,
    w_out_ref, w_up_ref, w_down_ref, w_mod_ref,
    velocity_ref,
    out_buf, up_buf, down_buf, mod_buf, state_out, state_in, mixed,
    first, first_in, spread, second, second_in, hidden, attended, units_own, columns, down_columns, key_rows, shift_rows,
    own_sem, y_send, y_recv, x_send, x_recv, core_send, core_recv, state_sems,
    first_send, first_recv, spread_send, spread_recv, second_send, second_recv,
):
    ranks, slabs, head_count, head_size, rows, tokens, quarters = sizes
    z = lax.axis_index("tensor")
    f = lax.axis_index("frame")
    pool = lax.axis_index("pool")
    core = lax.rem(pool, 2)
    other_core = pool + 1 - 2 * core
    other_chip = lax.rem(pool + 2, 4)
    other_f = 1 - f
    factor = head_size ** (-0.5)

    barrier = pltpu.get_barrier_semaphore()
    pl.semaphore_signal(barrier, inc=1, device_id={"frame": other_f}, device_id_type=MESH)
    pl.semaphore_signal(barrier, inc=1, device_id={"pool": other_core}, device_id_type=MESH)
    pl.semaphore_signal(barrier, inc=1, device_id={"pool": other_chip}, device_id_type=MESH)

    @pl.when(z > 0)
    def _():
        pl.semaphore_signal(barrier, inc=1, device_id={"tensor": z - 1}, device_id_type=MESH)

    @pl.when(z < ranks - 1)
    def _():
        pl.semaphore_signal(barrier, inc=1, device_id={"tensor": z + 1}, device_id_type=MESH)

    sources = (w_out_ref, w_up_ref, w_down_ref)
    buffers = (out_buf, up_buf, down_buf)
    own_copies = [
        pltpu.make_async_copy(sources[i], buffers[i].at[f], own_sem.at[i]) for i in range(3)
    ]
    for copy in own_copies:
        copy.start()
    mod_copy = pltpu.make_async_copy(w_mod_ref, mod_buf, own_sem.at[3])
    mod_copy.start()

    earlier = (
        lax.broadcasted_iota(jnp.int32, (tokens, tokens), 0)
        <= lax.broadcasted_iota(jnp.int32, (tokens, tokens), 1)
    ).astype(jnp.float32).astype(jnp.bfloat16)
    rest = decay_ref[...]
    cum = jnp.zeros_like(rest)
    for _ in range(3):
        leading = rest.astype(jnp.bfloat16)
        rest = rest - leading.astype(jnp.float32)
        cum += jnp.dot(leading, earlier, preferred_element_type=jnp.float32)
    columns[...] = jnp.zeros_like(columns)
    columns[0:head_count, :] = cum
    columns[head_count : head_count + 1, :] = label_ref[...].astype(jnp.float32)
    down_columns[...] = columns[...].T

    for h in range(head_count):
        part = slice(h * head_size, (h + 1) * head_size)
        row = cum[h : h + 1, :]
        total = row[:, tokens - 1 : tokens]
        keys = k_ref[part, :].astype(jnp.float32)
        key_rows[h] = keys.T.astype(jnp.bfloat16)
        scaled = (keys * jnp.exp(total - row)).astype(jnp.bfloat16)
        state_out[h] = lax.dot_general(
            v_ref[part, :], scaled, (((1,), (1,)), ((), ())), preferred_element_type=jnp.float32
        ).astype(jnp.bfloat16)

    links = 3 + (z > 0).astype(jnp.int32) + (z < ranks - 1).astype(jnp.int32)
    pl.semaphore_wait(barrier, links)

    state_copy = pltpu.make_async_remote_copy(
        src_ref=state_out, dst_ref=state_in, send_sem=state_sems.at[0], recv_sem=state_sems.at[1],
        device_id={"frame": other_f}, device_id_type=MESH,
    )

    @pl.when(f == 0)
    def _():
        state_copy.start()
        state_in[...] = jnp.zeros_like(state_in)

    def across(i, quarter):
        part = pl.ds(*quarters[i][quarter])
        return pltpu.make_async_remote_copy(
            src_ref=sources[i].at[part], dst_ref=buffers[i].at[f, part],
            send_sem=y_send.at[i], recv_sem=y_recv.at[i],
            device_id={"frame": other_f}, device_id_type=MESH,
        )

    def arrived(i, quarter):
        part = pl.ds(*quarters[i][quarter])
        return pltpu.make_async_remote_copy(
            src_ref=sources[i].at[part], dst_ref=buffers[i].at[other_f, part],
            send_sem=y_send.at[i], recv_sem=y_recv.at[i],
            device_id={"frame": other_f}, device_id_type=MESH,
        )

    def region(i, quarter):
        return buffers[i].at[other_f, pl.ds(*quarters[i][quarter])]

    def to_chip(i, quarter):
        return pltpu.make_async_remote_copy(
            src_ref=region(i, quarter), dst_ref=region(i, quarter),
            send_sem=x_send.at[i], recv_sem=x_recv.at[i],
            device_id={"pool": other_chip}, device_id_type=MESH,
        )

    def to_core(i, quarter, turn):
        return pltpu.make_async_remote_copy(
            src_ref=region(i, quarter), dst_ref=region(i, quarter),
            send_sem=core_send.at[i, turn], recv_sem=core_recv.at[i, turn],
            device_id={"pool": other_core}, device_id_type=MESH,
        )

    def each_quarter(act):
        for quarter in range(4):
            @pl.when(pool == quarter)
            def _():
                act(quarter)

    each_quarter(lambda quarter: across(0, quarter).start())

    def pass_on(i):
        def act(quarter):
            arrived(i, quarter).wait_recv()
            to_chip(i, quarter).start()
            to_core(i, quarter, 0).start()
        each_quarter(act)

    def pass_round(i):
        def act(quarter):
            opposite = (quarter + 2) % 4
            to_chip(i, opposite).wait_recv()
            to_core(i, opposite, 1).start()
        each_quarter(act)

    def settle(i):
        def act(quarter):
            to_core(i, quarter ^ 1, 0).wait_recv()
            to_core(i, (quarter ^ 1) ^ 2, 1).wait_recv()
        each_quarter(act)

    @pl.when(f > 0)
    def _():
        state_copy.wait_recv()

    def attend(d):
        block = pl.ds(pl.multiple_of(d * rows, rows), rows)
        visible = (
            down_columns[:, head_count : head_count + 1] <= columns[head_count : head_count + 1, block]
        )
        for h in range(head_count):
            part = slice(h * head_size, (h + 1) * head_size)
            qh = q_ref[part, block]
            scores = jnp.dot(key_rows[h], qh, preferred_element_type=jnp.float32)
            row = columns[h : h + 1, block]
            decay = jnp.exp(jnp.minimum(row - down_columns[:, h : h + 1], 0.0))
            probs = (scores * (jnp.where(visible, decay, 0.0) * factor)).astype(jnp.bfloat16)
            inner = jnp.dot(v_ref[part, :], probs, preferred_element_type=jnp.float32)
            carried = jnp.dot(state_in[h], qh, preferred_element_type=jnp.float32)
            numerator = inner + carried * (jnp.exp(row) * factor)
            power = jnp.mean(numerator * numerator, axis=0, keepdims=True)
            mixed[block, part] = (numerator * lax.rsqrt(power + 1e-06)).T.astype(jnp.bfloat16)

    own_copies[0].wait()

    def rows_of(d):
        return pl.ds(pl.multiple_of(d * rows, rows), rows)

    def hop(buf, landing, send_sem, recv_sem, way, d, s):
        to = at_most(ranks, z + 1 - 2 * way)
        return pltpu.make_async_remote_copy(
            src_ref=buf.at[d, s], dst_ref=landing.at[way, d, s],
            send_sem=send_sem.at[d, s], recv_sem=recv_sem.at[way, d, s],
            device_id={"tensor": to}, device_id_type=MESH,
        )

    def hop1(way, d, s):
        return hop(first, first_in, first_send, first_recv, way, d, s)

    shares = second_send.shape[2]

    def share(r):
        return pl.ds(r * (rows // shares), rows // shares)

    def hop2(way, d, s, r):
        to = at_most(ranks, z + 1 - 2 * way)
        return pltpu.make_async_remote_copy(
            src_ref=second.at[d, s, share(r)], dst_ref=second_in.at[way, d, s, share(r)],
            send_sem=second_send.at[d, s, r], recv_sem=second_recv.at[way, d, s, r],
            device_id={"tensor": to}, device_id_type=MESH,
        )

    def has_upstream(way):
        return jnp.where(way == 0, z > 0, z < ranks - 1)

    def first_turn(turn, s, fresh):
        step = turn // 2
        near = jnp.where(z < ranks // 2, 0, 1)
        way = lax.rem(turn + near, 2)
        d = jnp.where(way == 0, ranks - 1 - step, step)
        active = jnp.where(way == 0, d > z, d < z)

        @pl.when(active)
        def _():
            if fresh:
                attend(d)
            part = jnp.dot(mixed[rows_of(d), :], out_buf[s], preferred_element_type=jnp.float32)
            first[d, s] = part.astype(jnp.bfloat16)

            @pl.when(has_upstream(way))
            def _():
                hop1(way, d, s).wait_recv()
                first[d, s] = (
                    first[d, s].astype(jnp.float32) + first_in[way, d, s].astype(jnp.float32)
                ).astype(jnp.bfloat16)

            hop1(way, d, s).start()

    def own_slab(s):
        part = jnp.dot(mixed[rows_of(z), :], out_buf[s], preferred_element_type=jnp.float32)
        attended[s] = part.astype(jnp.bfloat16).astype(jnp.float32)

    def near_columns(turn, carry):
        first_turn(turn, f, True)

        @pl.when(turn == ranks // 2 - 1)
        def _():
            pass_on(0)
            each_quarter(lambda quarter: across(1, quarter).start())

        @pl.when(turn == ranks - 1)
        def _():
            pass_round(0)
            each_quarter(lambda quarter: across(2, quarter).start())

        return carry

    lax.fori_loop(0, 2 * (ranks - 1), near_columns, 0)
    attend(z)
    own_slab(f)
    settle(0)

    def far_columns(turn, carry):
        first_turn(turn, other_f, False)

        @pl.when(turn == 1)
        def _():
            pass_on(1)

        return carry

    lax.fori_loop(0, 2 * (ranks - 1), far_columns, 0)
    own_slab(other_f)

    mod_copy.wait()
    shift_rows[...] = jnp.dot(feature_ref[...], mod_buf[...], preferred_element_type=jnp.float32)
    piece = hidden.shape[2]

    def shift(kind, s):
        start = (kind * slabs + s) * piece
        return shift_rows[0:1, start : start + piece]

    def lat(s):
        return lat_ref[s * piece : (s + 1) * piece, :].astype(jnp.float32).T

    for way in range(2):
        @pl.when(has_upstream(way))
        def _():
            for s in range(slabs):
                hop1(way, z, s).wait_recv()
                attended[s] += first_in[way, z, s].astype(jnp.float32)

    total = jnp.zeros((rows, 1), jnp.float32)
    for s in range(slabs):
        value = lat(s) + shift(3, s) * attended[s]
        hidden[s] = value
        total += jnp.sum(value, axis=1, keepdims=True)
    width = slabs * hidden.shape[2]
    mean = total / width
    squares = jnp.zeros((rows, 1), jnp.float32)
    for s in range(slabs):
        centered = hidden[s] - mean
        squares += jnp.sum(centered * centered, axis=1, keepdims=True)
    inverse = lax.rsqrt(squares / width + 1e-06)
    for s in range(slabs):
        spread[z, s] = (
            (hidden[s] - mean) * inverse * (1.0 + shift(1, s)) + shift(0, s)
        ).astype(jnp.bfloat16)

    def relay(way, c, s):
        to = at_most(ranks, z + 1 - 2 * way)
        return pltpu.make_async_remote_copy(
            src_ref=spread.at[c, s], dst_ref=spread.at[c, s],
            send_sem=spread_send.at[way, c, s], recv_sem=spread_recv.at[c, s],
            device_id={"tensor": to}, device_id_type=MESH,
        )

    def has_downstream(way):
        return jnp.where(way == 0, z < ranks - 1, z > 0)

    for way in range(2):
        @pl.when(has_downstream(way))
        def _():
            for s in range(slabs):
                relay(way, z, s).start()

    pass_round(1)
    pass_on(2)
    own_copies[1].wait()
    settle(1)

    def up_side(c):
        acc = jnp.dot(spread[c, 0], up_buf[0], preferred_element_type=jnp.float32)
        for s in range(1, slabs):
            acc += jnp.dot(spread[c, s], up_buf[s], preferred_element_type=jnp.float32)
        return jax.nn.gelu(acc, approximate=True).astype(jnp.bfloat16)

    units_own[...] = up_side(z)

    def tick(k, carry):
        def chunk_of(way):
            return jnp.where(way == 0, z - k, z + k)

        def arrival(turn, c0):
            s, way = turn // 2, lax.rem(turn, 2)
            c = chunk_of(way)

            @pl.when((c >= 0) & (c < ranks))
            def _():
                relay(way, c, s).wait_recv()

                @pl.when(has_downstream(way))
                def _():
                    relay(way, c, s).start()

            return c0

        def work(way, c0):
            c = chunk_of(way)

            @pl.when((c >= 0) & (c < ranks))
            def _():
                units = up_side(c)

                @pl.when((k == 1) & ((way == 0) | (z == 0)))
                def _():
                    own_copies[2].wait()
                    pass_round(2)
                    settle(2)

                for s in range(slabs):
                    second[c, s] = jnp.dot(
                        units, down_buf[s], preferred_element_type=jnp.float32
                    ).astype(jnp.bfloat16)

                    @pl.when(jnp.logical_not(has_upstream(1 - way)))
                    def _():
                        for r in range(shares):
                            hop2(1 - way, c, s, r).start()

            return c0

        @pl.when(k < ranks)
        def _():
            lax.fori_loop(0, 2 * slabs, arrival, 0)
            lax.fori_loop(0, 2, work, 0)

        def sending(way, c0):
            place = jnp.where(way == 0, z, ranks - 1 - z)
            ahead = k - place
            d = jnp.where(way == 0, ahead, ranks - 1 - ahead)

            @pl.when((place > 0) & (ahead > place) & (ahead < ranks))
            def _():
                def slab(s, c1):
                    for r in range(shares):
                        hop2(way, d, s, r).wait_recv()
                        second[d, s, share(r)] = (
                            second[d, s, share(r)].astype(jnp.float32)
                            + second_in[way, d, s, share(r)].astype(jnp.float32)
                        ).astype(jnp.bfloat16)
                        hop2(way, d, s, r).start()
                    return c1

                lax.fori_loop(0, slabs, slab, 0)

            return c0

        lax.fori_loop(0, 2, sending, 0)
        return carry

    lax.fori_loop(1, 2 * ranks - 2, tick, 0)

    for s in range(slabs):
        attended[s] = (
            jnp.dot(units_own[...], down_buf[s], preferred_element_type=jnp.float32)
            .astype(jnp.bfloat16)
            .astype(jnp.float32)
        )
    for way in range(2):
        @pl.when(has_upstream(way))
        def _():
            for s in range(slabs):
                for r in range(shares):
                    hop2(way, z, s, r).wait_recv()
                attended[s] += second_in[way, z, s].astype(jnp.float32)
    for s in range(slabs):
        velocity = hidden[s] + shift(2, s) * attended[s]
        velocity_ref[s * piece : (s + 1) * piece, :] = velocity.T

    @pl.when(f == 0)
    def _():
        state_copy.wait_send()

    for i in range(3):
        def left(quarter):
            across(i, quarter).wait_send()
            to_chip(i, quarter).wait_send()
            to_core(i, quarter, 0).wait_send()
            to_core(i, (quarter + 2) % 4, 1).wait_send()
        each_quarter(left)

    def drain(d, carry):
        def slab(s, c):
            @pl.when(d != z)
            def _():
                way = jnp.where(d > z, 0, 1)
                hop1(way, d, s).wait_send()
                for r in range(shares):
                    hop2(way, d, s, r).wait_send()

            def direction(way, c1):
                came = jnp.where(way == 0, d <= z, d >= z)

                @pl.when(came & has_downstream(way))
                def _():
                    relay(way, d, s).wait_send()

                return c1

            lax.fori_loop(0, 2, direction, 0)
            return c

        lax.fori_loop(0, slabs, slab, 0)
        return carry

    lax.fori_loop(0, ranks, drain, 0)


def fits(latents, queries, log_decay, w_out, w_up, w_down):
    frames, ranks, pools = (lax.axis_size(a) for a in ("frame", "tensor", "pool"))
    rows, tokens = latents.shape[0], queries.shape[0]
    return (
        frames == 2
        and pools == 4
        and ranks > 1
        and rows % 128 == 0
        and latents.shape[1] % (16 * frames) == 0
        and log_decay.shape[0] < 8
        and rows * ranks == tokens
        and rows % 16 == 0
        and all(w.shape[0] % 16 == 0 and w.shape[0] >= 64 for w in (w_out, w_up, w_down))
        and w_up.shape[0] == w_out.shape[1] == w_down.shape[1]
        and queries.shape[1] // log_decay.shape[0] % 16 == 0
    )


def on_device(
    latents, queries, keys, values, log_decay, block_ids, t_index, w_mod, w_out, w_up, w_down
):
    if not fits(latents, queries, log_decay, w_out, w_up, w_down):
        return by_collectives(
            latents, queries, keys, values, log_decay, block_ids, t_index, w_mod, w_out, w_up, w_down
        )
    ranks, slabs = lax.axis_size("tensor"), lax.axis_size("frame")
    rows, width = latents.shape
    piece = width // slabs
    tokens, features = queries.shape
    head_count = log_decay.shape[0]
    head_size = features // head_count
    time_features, step_size = time_embedding(t_index, w_mod)

    def split(count):
        edges = [count // 16 * i // 4 * 16 for i in range(5)]
        return tuple((edges[i], edges[i + 1] - edges[i]) for i in range(4))

    quarters = tuple(split(w.shape[0]) for w in (w_out, w_up, w_down))
    sizes = (ranks, slabs, head_count, head_size, rows, tokens, quarters)
    block = (ranks, slabs, rows, piece)
    vmem = pl.BlockSpec(memory_space=pltpu.VMEM)
    anywhere = pl.BlockSpec(memory_space=pl.ANY)
    dma = pltpu.SemaphoreType.DMA
    velocity = pl.pallas_call(
        functools.partial(fused, sizes),
        out_shape=jax.ShapeDtypeStruct((width, rows), jnp.float32),
        in_specs=[vmem] * 7 + [anywhere] * 4,
        out_specs=vmem,
        scratch_shapes=[
            pltpu.VMEM((slabs,) + w_out.shape, jnp.bfloat16),
            pltpu.VMEM((slabs,) + w_up.shape, jnp.bfloat16),
            pltpu.VMEM((slabs,) + w_down.shape, jnp.bfloat16),
            pltpu.VMEM(w_mod.shape, jnp.bfloat16),
            pltpu.VMEM((head_count, head_size, head_size), jnp.bfloat16),
            pltpu.VMEM((head_count, head_size, head_size), jnp.bfloat16),
            pltpu.VMEM((tokens, features), jnp.bfloat16),
            pltpu.VMEM(block, jnp.bfloat16),
            pltpu.VMEM((2,) + block, jnp.bfloat16),
            pltpu.VMEM(block, jnp.bfloat16),
            pltpu.VMEM(block, jnp.bfloat16),
            pltpu.VMEM((2,) + block, jnp.bfloat16),
            pltpu.VMEM((slabs, rows, piece), jnp.float32),
            pltpu.VMEM((slabs, rows, piece), jnp.float32),
            pltpu.VMEM((rows, w_up.shape[1]), jnp.bfloat16),
            pltpu.VMEM((8, tokens), jnp.float32),
            pltpu.VMEM((tokens, 8), jnp.float32),
            pltpu.VMEM((head_count, tokens, head_size), jnp.bfloat16),
            pltpu.VMEM((8, w_mod.shape[1]), jnp.float32),
            dma((4,)), dma((3,)), dma((3,)), dma((3,)), dma((3,)), dma((3, 2)), dma((3, 2)), dma((2,)),
            dma((ranks, slabs)), dma((2, ranks, slabs)),
            dma((2, ranks, slabs)), dma((ranks, slabs)),
            dma((ranks, slabs, 4)), dma((2, ranks, slabs, 4)),
        ],
        compiler_params=pltpu.CompilerParams(
            collective_id=0, has_side_effects=True, vmem_limit_bytes=56 * 1024 * 1024
        ),
        name="sublayers",
    )(
        queries.T, keys.T, values.T, log_decay, block_ids[None, :], latents.T,
        jnp.broadcast_to(time_features, (8, time_features.shape[0])),
        w_out, w_up, w_down, w_mod,
    )
    velocity = velocity.T.astype(jnp.bfloat16)
    advanced = latents.astype(jnp.float32) + step_size * velocity.astype(jnp.float32)
    return (velocity, advanced.astype(jnp.bfloat16))


def solution(mesh):
    return jax.shard_map(
        on_device,
        mesh=mesh,
        in_specs=(
            P(("pool", "frame", "tensor"), None),
            P(("pool", "frame"), "tensor"),
            P(("pool", "frame"), "tensor"),
            P(("pool", "frame"), "tensor"),
            P("tensor", ("pool", "frame")),
            P(("pool", "frame")),
            P("pool"),
            P(),
            P("tensor", "frame"),
            P("frame", "tensor"),
            P("tensor", "frame"),
        ),
        out_specs=(P(("pool", "frame", "tensor"), None), P(("pool", "frame", "tensor"), None)),
        check_vma=False,
    )
```
